32 devices in a mesh: grp: 2 (over x), tp: 16 (over z, y, core).
Axes of the slice: x: 2, y: 2, z: 4, core: 2. Of those that a mesh axis runs over, the one named last changes fastest.
Arguments:
- residual_input: bfloat16 [256, 5120], P('grp', 'tp'), may hold values from -6 to 6
- input_norm_gain: float32 [5120], replicated, may hold values from 0.1 to 1.9
- query_weight: bfloat16 [5120, 4096], P(None, 'tp'), may hold values from -0.078125 to 0.078125
- key_value_weight: bfloat16 [5120, 1024], P(None, 'tp'), may hold values from -0.3125 to 0.3125
- shared_down_factors: bfloat16 [5120, 48], replicated, may hold values from -0.078125 to 0.078125
- query_up_factors: bfloat16 [16, 16, 4096], P(None, None, 'tp'), may hold values from -1 to 1
- key_value_up_factors: bfloat16 [16, 16, 1024], replicated, may hold values from -1 to 1
- paged_base_keys: bfloat16 [128, 128, 512], P(('grp', 'tp')), may hold values from -100 to 100
- paged_base_values: bfloat16 [128, 128, 512], P(('grp', 'tp')), may hold values from -6 to 6
- paged_down_factors: bfloat16 [128, 128, 32], P(('grp', 'tp')), may hold values from -6 to 6
- adapter_of_row: int32 [256], P('grp'), may hold values from 0 to 15
- document_of_row: int32 [256, 1], P('grp'), may hold values from 0 to 1; in each aligned block of 128 rows (0 to 127, 128 to 255, ...) at most 128 rows name the same one
- document_page_slots: int32 [2, 64], replicated, may hold values from 0 to 127, as said below
Outputs:
- attended: bfloat16 [256, 4096], P('grp', 'tp')
The draws below stay inside these ranges and needn't reach their ends.
Inputs may be any that keep to these rules, and one draw needn't show every extreme that they name: `document_of_row`: in each aligned block of 128 rows no document is named by more than 128 rows. `document_page_slots`: each page slot is used once; all pages of one document lie on the 16 devices of one index of grp, 4 on each, documents and indices of grp one to one.
All inputs are finite; a program needn't handle non-finite values.
Results may differ from the reference program's by a relative error of at most 0.034.
Values may be sent and summed in bfloat16 or wider, within the bound.
A program may use at most 64 MiB of HBM per device.

```python
import math
import jax
import jax.numpy as jnp
import numpy as np
from jax import lax

MODEL_WIDTH = 5120
QH = 32
KEY_VALUE_HEADS = 4
HEAD_SIZE = 128
UPDATE_RANK = 16
PAGE = 128
ADAPTER_COUNT = 16
ROWS_GRP = 128
QUERY_WIDTH = 4096
KEY_WIDTH = 512
ROWS = 256
DOCS = 2
DOC_PAGES = 64
CTX = 8192
TOTAL_PAGES = 128
CAP = 128


def draw_document_page_slots(key, part):
    key = jax.random.fold_in(key, 5)
    first_key, second_key = jax.random.split(key)
    group_of_doc = jax.random.permutation(first_key, DOCS)
    doc_keys = jax.random.split(second_key, DOCS)
    within = jax.vmap(lambda one_key: jax.random.permutation(one_key, DOC_PAGES))(doc_keys)
    return (group_of_doc[:, None] * DOC_PAGES + within).astype(jnp.int32)


def draw_paged_base_keys(key, part):
    key = jax.random.fold_in(key, 9)
    base_key = jax.random.fold_in(key, 0)
    array_shape = (TOTAL_PAGES, PAGE, KEY_WIDTH)
    base_keys = 2.5 * jax.random.normal(base_key, array_shape, jnp.float32)
    return jnp.clip(base_keys, -100.0, 100.0).astype(jnp.bfloat16)


def set_ends(drawn, key, smallest, largest):
    place = [jax.random.randint(jax.random.fold_in(key, axis), (), 0, length) for axis, length in enumerate(drawn.shape)]
    widest = drawn.shape.index(max(drawn.shape))
    beside = place[:widest] + [(place[widest] + 1) % drawn.shape[widest]] + place[widest + 1:]
    return drawn.at[tuple(place)].set(smallest).at[tuple(beside)].set(largest)


def shard_levels(stream_key, dims, cuts, smallest, largest):
    def one(dim, blocks):
        draws = jax.random.uniform(jax.random.fold_in(jax.random.fold_in(stream_key, 6), dim), (blocks,), jnp.float32, smallest / len(cuts), largest / len(cuts))
        return jnp.repeat(jnp.exp(draws), dims[dim] // blocks).reshape((-1,) + (1,) * (len(dims) - dim - 1))

    loudness = one(*cuts[0])
    for cut in cuts[1:]:
        loudness = loudness * one(*cut)
    return loudness


def rank_bounds(amount, slope):
    portions = [(1 << 20) // math.isqrt(rank ** slope) + 1 for rank in range(1, amount + 1)]
    deviation = 1 + sum(portions) // (1 << 30)
    return np.cumsum(np.array([max(1, weight // deviation) for weight in portions]))


def ranked(rng, dims, count, lean):
    grid = rank_bounds(count, lean)
    ticket = jax.random.randint(jax.random.fold_in(rng, 1), dims, 0, int(grid[count - 1]))
    grade = jnp.searchsorted(jnp.asarray(grid, jnp.int32), ticket, side="right")
    return jax.random.permutation(jax.random.fold_in(rng, 2), count)[grade].astype(jnp.int32)


def routed_block(key, own, number, rows, number_of, top, most, skew):
    ranking = jax.random.permutation(key, number_of)
    crowded, common = portions_of(number_of, rows * top, most, skew, True), portions_of(number_of, rows * top, most, skew, False)
    places = jnp.arange(number_of)

    def named(tallies, turn):
        used = int((tallies > 0).sum())
        fixed = max(1, used // 4)
        moved = fixed + (places - fixed + turn * (used - fixed)) % max(1, number_of - fixed)
        return jnp.zeros((number_of,), jnp.int32).at[ranking[jnp.where(places < fixed, places, moved)]].set(jnp.asarray(tallies, jnp.int32))

    tallies = jnp.where(number % 4 == 0, named(crowded, number // 4), named(common, number - number // 4 - 1))
    mixed = jax.random.permutation(jax.random.fold_in(own, 3), number_of)
    donor, sink = mixed[0:number_of // 2 * 2:2], mixed[1:number_of // 2 * 2:2]
    margin = jnp.minimum(tallies[donor] - 1, most - tallies[sink]) // 2
    margin = jnp.where((donor == ranking[0]) | (sink == ranking[0]) | (tallies[sink] == 0), 0, jnp.maximum(margin, 0))
    moved = jax.random.randint(jax.random.fold_in(own, 4), (number_of // 2,), 0, 1 << 20) % (margin + 1)
    tallies = tallies.at[donor].add(-moved).at[sink].add(moved)
    labels = jnp.searchsorted(jnp.cumsum(tallies), jnp.arange(rows * top), side="right").astype(jnp.int32)
    table = labels.reshape(top, rows).T
    table = table[jax.random.permutation(jax.random.fold_in(own, 1), rows)]
    turn = jax.random.randint(jax.random.fold_in(own, 2), (rows, 1), 0, top)
    return jnp.take_along_axis(table, (jnp.arange(top)[None, :] + turn) % top, axis=1)


def portions_of(amount, total, reach, slope, full):
    loads = [(1 << 20) // math.isqrt(grade ** slope) + 1 for grade in range(1, amount + 1)]
    largest = reach if full else min(reach, max(-(-total // amount), total * loads[0] // sum(loads)))
    least = 1 if total - largest >= amount - 1 else 0
    given, spare = [largest] + [least] * (amount - 1), total - largest - least * (amount - 1)
    while spare > 0:
        movable = [i for i in range(1, amount) if given[i] < largest] or [i for i in range(1, amount) if given[i] < reach]
        pool, remaining = sum([loads[i] for i in movable]), spare
        for i in movable:
            addition = min(reach - given[i], max(1, remaining * loads[i] // pool), spare)
            given[i] = given[i] + addition
            spare = spare - addition
    return np.array(given)


def bell_draw(rng, extent, spread, limit, cuts=(), dtype=jnp.bfloat16):
    drawn = spread * jax.random.normal(rng, extent, jnp.float32)
    if cuts:
        drawn = drawn * shard_levels(rng, extent, cuts, -0.22, 0.18)
    return jnp.clip(drawn, -limit, limit).astype(dtype)


def setup_inputs(seed: int = 0) -> dict:
    arg_keys = jax.random.split(jax.random.key(seed), 14)
    residual_input = bell_draw(arg_keys[0], (ROWS, MODEL_WIDTH), 1.0, 6.0, ((0, 2), (1, 16)))
    input_norm_gain = jnp.clip(1.0 + 0.18 * jax.random.normal(arg_keys[1], (MODEL_WIDTH,), jnp.float32), 0.1, 1.9)
    query_weight = bell_draw(arg_keys[2], (MODEL_WIDTH, QUERY_WIDTH), MODEL_WIDTH ** -0.5, 0.078125, ((1, 16),))
    key_value_weight = bell_draw(arg_keys[3], (MODEL_WIDTH, 2 * KEY_WIDTH), (MODEL_WIDTH // 12) ** -0.5, 0.3125, ((1, 16),))
    shared_down_factors = bell_draw(arg_keys[4], (MODEL_WIDTH, 3 * UPDATE_RANK), MODEL_WIDTH ** -0.5, 0.078125)
    query_up_factors = bell_draw(arg_keys[5], (ADAPTER_COUNT, UPDATE_RANK, QUERY_WIDTH), 0.125, 1.0, ((2, 16),))
    key_value_up_factors = bell_draw(arg_keys[6], (ADAPTER_COUNT, UPDATE_RANK, 2 * KEY_WIDTH), 0.125, 1.0)
    paged_base_keys = draw_paged_base_keys(jax.random.fold_in(arg_keys[13], 71), 0)
    paged_base_values = bell_draw(arg_keys[8], (TOTAL_PAGES, PAGE, KEY_WIDTH), 1.0, 6.0, ((0, 32),))
    paged_down_factors = bell_draw(arg_keys[9], (TOTAL_PAGES, PAGE, 2 * UPDATE_RANK), 1.0, 6.0, ((0, 32),))
    adapter_of_row = set_ends(ranked(arg_keys[10], (ROWS,), ADAPTER_COUNT, 2), jax.random.fold_in(arg_keys[10], 3), 0, ADAPTER_COUNT - 1).astype(jnp.int32)
    document_of_row_keys = jax.random.split(jax.random.fold_in(arg_keys[11], 1), ROWS // ROWS_GRP)
    document_of_row_turns = jax.random.permutation(jax.random.fold_in(arg_keys[11], 3), ROWS // ROWS_GRP)
    document_of_row = jax.vmap(lambda own, number: routed_block(jax.random.fold_in(arg_keys[11], 2), own, number, ROWS_GRP, DOCS, 1, CAP, 2))(document_of_row_keys, document_of_row_turns).reshape((ROWS, 1))
    document_page_slots = draw_document_page_slots(jax.random.fold_in(arg_keys[13], 71), 0)
    return {"residual_input": residual_input, "input_norm_gain": input_norm_gain, "query_weight": query_weight, "key_value_weight": key_value_weight, "shared_down_factors": shared_down_factors, "query_up_factors": query_up_factors, "key_value_up_factors": key_value_up_factors, "paged_base_keys": paged_base_keys, "paged_base_values": paged_base_values, "paged_down_factors": paged_down_factors, "adapter_of_row": adapter_of_row, "document_of_row": document_of_row, "document_page_slots": document_page_slots}


def reference(residual_input, input_norm_gain, query_weight, key_value_weight, shared_down_factors, query_up_factors, key_value_up_factors, paged_base_keys, paged_base_values, paged_down_factors, adapter_of_row, document_of_row, document_page_slots):
    single_row = jnp.float32
    half_width = jnp.bfloat16
    widened = residual_input.astype(single_row)
    normed_input = (widened * lax.rsqrt(lax.optimization_barrier(jnp.mean(widened * widened, -1, keepdims=True)) + 1e-06) * input_norm_gain).astype(half_width)
    low_rank_part = jnp.dot(normed_input, shared_down_factors, preferred_element_type=single_row).astype(half_width)
    query_low_rank = low_rank_part[:, :UPDATE_RANK]
    key_low_rank = low_rank_part[:, UPDATE_RANK:2 * UPDATE_RANK]
    value_low_rank = low_rank_part[:, 2 * UPDATE_RANK:]
    query_total = jnp.dot(normed_input, query_weight, preferred_element_type=single_row)
    key_total = jnp.dot(normed_input, key_value_weight[:, :KEY_WIDTH], preferred_element_type=single_row)
    value_total = jnp.dot(normed_input, key_value_weight[:, KEY_WIDTH:], preferred_element_type=single_row)
    for adapter_index in range(ADAPTER_COUNT):
        picked_factors = (adapter_of_row == adapter_index)[:, None]
        query_total = query_total + jnp.where(picked_factors, jnp.dot(query_low_rank, query_up_factors[adapter_index], preferred_element_type=single_row), 0.0)
        key_total = key_total + jnp.where(picked_factors, jnp.dot(key_low_rank, key_value_up_factors[adapter_index][:, :KEY_WIDTH], preferred_element_type=single_row), 0.0)
        value_total = value_total + jnp.where(picked_factors, jnp.dot(value_low_rank, key_value_up_factors[adapter_index][:, KEY_WIDTH:], preferred_element_type=single_row), 0.0)
    query_matrix = query_total.astype(half_width)
    fresh_key = key_total.astype(half_width)
    fresh_value = value_total.astype(half_width)
    query_group_size = QH // KEY_VALUE_HEADS
    query_wide = query_matrix.astype(single_row).reshape(ROWS, KEY_VALUE_HEADS, query_group_size, HEAD_SIZE)
    factor_sum = jnp.zeros((ROWS, KEY_VALUE_HEADS, query_group_size, UPDATE_RANK), single_row)
    for adapter_index in range(ADAPTER_COUNT):
        picked_wide = (adapter_of_row == adapter_index)[:, None, None, None]
        key_projected = key_value_up_factors[adapter_index][:, :KEY_WIDTH].astype(single_row).reshape(UPDATE_RANK, KEY_VALUE_HEADS, HEAD_SIZE)
        factor_sum = factor_sum + jnp.where(picked_wide, jnp.einsum('rkgd,jkd->rkgj', query_wide, key_projected), 0.0)
    down_factors = factor_sum.astype(half_width)
    value_update = key_value_up_factors[adapter_of_row][:, :, KEY_WIDTH:]
    row_page_block = 8
    page_block_count = ROWS // row_page_block
    score_scaling = HEAD_SIZE ** (-0.5)

    def attend(bundle):
        query_rows, factor_rows, own_key, value_own, value_up, doc_ids = bundle
        page_ids = document_page_slots[doc_ids]
        key_block = paged_base_keys[page_ids].reshape(row_page_block, CTX, KEY_VALUE_HEADS, HEAD_SIZE).astype(single_row)
        value_block = paged_base_values[page_ids].reshape(row_page_block, CTX, KEY_VALUE_HEADS, HEAD_SIZE).astype(single_row)
        cached = paged_down_factors[page_ids].reshape(row_page_block, CTX, 2 * UPDATE_RANK).astype(single_row)
        query_head_count = query_rows.astype(single_row).reshape(row_page_block, KEY_VALUE_HEADS, query_group_size, HEAD_SIZE)
        factor_heads = factor_rows.astype(single_row)
        scores = (jnp.einsum('bkgd,btkd->bkgt', query_head_count, key_block) + jnp.einsum('bkgj,btj->bkgt', factor_heads, cached[..., :UPDATE_RANK])) * score_scaling
        own_token_score = jnp.einsum('amzu,amu->amz', query_head_count, own_key.astype(single_row).reshape(row_page_block, KEY_VALUE_HEADS, HEAD_SIZE)) * score_scaling
        peak_all = jnp.maximum(lax.optimization_barrier(jnp.max(scores, -1)), own_token_score)
        weights = jnp.exp(scores - peak_all[..., None])
        own_weight = jnp.exp(own_token_score - peak_all)
        totals = lax.optimization_barrier(jnp.sum(weights, -1)) + own_weight
        rounded = lax.optimization_barrier(weights.astype(half_width)).astype(single_row)
        numerator = jnp.einsum('bkgt,btkd->bkgd', rounded, value_block) + own_weight[..., None] * value_own.astype(single_row).reshape(row_page_block, KEY_VALUE_HEADS, 1, HEAD_SIZE)
        low_sum = jnp.einsum('bkgt,btj->bkgj', rounded, cached[..., UPDATE_RANK:])
        value_shift = jnp.einsum('bkgj,bjkd->bkgd', low_sum, value_up.astype(single_row).reshape(row_page_block, UPDATE_RANK, KEY_VALUE_HEADS, HEAD_SIZE), precision=lax.Precision.HIGHEST)
        return ((numerator + value_shift) / totals[..., None]).astype(half_width).reshape(row_page_block, QH * HEAD_SIZE)
    factor_bundles = (query_matrix.reshape(page_block_count, row_page_block, QUERY_WIDTH), down_factors.reshape(page_block_count, row_page_block, KEY_VALUE_HEADS, query_group_size, UPDATE_RANK), fresh_key.reshape(page_block_count, row_page_block, KEY_WIDTH), fresh_value.reshape(page_block_count, row_page_block, KEY_WIDTH), value_update.reshape(page_block_count, row_page_block, UPDATE_RANK, KEY_WIDTH), document_of_row[:, 0].reshape(page_block_count, row_page_block))
    return lax.map(attend, factor_bundles).reshape(ROWS, QUERY_WIDTH)
```

```python
import functools
import math

import jax
import jax.numpy as jnp
from jax import lax
from jax.experimental import pallas as pl
from jax.experimental.pallas import tpu as pltpu
from jax.sharding import PartitionSpec as P

HEAD_SIZE = 128
MESH = pl.DeviceIdType.MESH
F32 = jnp.float32
BF16 = jnp.bfloat16


def dot(a, b):
    return jnp.dot(a, b, preferred_element_type=F32)


def dot_nt(a, b):
    return lax.dot_general(a, b, (((1,), (1,)), ((), ())), preferred_element_type=F32)


def lanes(shape):
    return lax.broadcasted_iota(jnp.int32, shape, len(shape) - 1)


def split_three(value):
    high = value.astype(BF16).astype(F32)
    middle = (value - high).astype(BF16).astype(F32)
    low = (value - high - middle).astype(BF16).astype(F32)
    return high, middle, low


def fused_kernel(
    x_ref, gain_ref, qw_hbm, kvw_hbm, dn_hbm, qu_ref, ku_ref, k_hbm, v_hbm, d_ref,
    adapter_ref, doc_ref, slots_ref, out_ref,
    xbuf, qw, kvw, dn, wo, yq, yo, ssq, kbuf, vbuf, dbuf, qbuf, lhs, kaug, vaug,
    acc, peak, psend, pbuf, fresh, fresh_in,
    load_sem, x_send, x_recv, kv_send, kv_recv, q_send, q_recv, f_send, f_recv, p_send, p_recv,
):
    rows = x_ref.shape[0]
    chunk = x_ref.shape[1]
    width = 16 * chunk
    grp = lax.axis_index("grp")
    tp = lax.axis_index("tp")
    z = tp // 4
    s = tp % 4
    y = s // 2
    c = s % 2
    scale = math.log2(math.e) / math.sqrt(HEAD_SIZE)

    def at(g, t):
        return {"grp": g, "tp": t}

    sibling = at(grp, z * 4 + y * 2 + (1 - c))
    across = at(grp, z * 4 + (1 - y) * 2 + c)
    z_others = [z + 1 - 2 * (z % 2), (z + 2) % 4, 3 - z]

    loads = [
        pltpu.make_async_copy(src, dst, load_sem.at[i])
        for i, (src, dst) in enumerate(
            ((kvw_hbm, kvw), (dn_hbm, dn), (qw_hbm, qw),
             (k_hbm.at[:, :, pl.ds(pl.multiple_of(z * 128, 128), 128)], kbuf.at[z]),
             (v_hbm.at[:, :, pl.ds(pl.multiple_of(z * 128, 128), 128)], vbuf.at[z]))
        )
    ]
    for load in loads:
        load.start()

    barrier = pltpu.get_barrier_semaphore()
    for i in range(1, 16):
        pl.semaphore_signal(barrier, inc=1, device_id=at(grp, (tp + i) % 16), device_id_type=MESH)
    for j in range(4):
        pl.semaphore_signal(barrier, inc=1, device_id=at(1 - grp, z * 4 + j), device_id_type=MESH)
    xbuf[tp] = x_ref[...]
    dbuf[z] = jnp.concatenate([d_ref[p] for p in range(4)], axis=1)
    pl.semaphore_wait(barrier, 19)

    started = []

    def send(src, dst, send_sem, recv_sem, device):
        copy = pltpu.make_async_remote_copy(
            src_ref=src, dst_ref=dst, send_sem=send_sem, recv_sem=recv_sem,
            device_id=device, device_id_type=MESH,
        )
        copy.start()
        return copy

    def arrive(dst, send_sem, recv_sem):
        pltpu.make_async_remote_copy(
            src_ref=dst, dst_ref=dst, send_sem=send_sem, recv_sem=recv_sem,
            device_id=sibling, device_id_type=MESH,
        ).wait_recv()

    def send_x(t, sem, device):
        copy = send(xbuf.at[t], xbuf.at[t], x_send.at[sem], x_recv.at[t], device)
        started.append(copy)
        return copy

    first = [send_x(tp, i, at(grp, zo * 4 + s)) for i, zo in enumerate(z_others)]
    send_x(tp, 3, across)
    send_x(tp, 7, sibling)

    loads[0].wait()
    loads[1].wait()

    def join(i, carry):
        part = pl.ds(pl.multiple_of(i * chunk, 64), chunk)
        wo[part, :] = jnp.concatenate(
            [kvw[part, :], dn[part, :], jnp.zeros((chunk, 16), BF16)], axis=1
        )
        return carry

    lax.fori_loop(0, 16, join, 0)
    yq[...] = jnp.zeros_like(yq)
    yo[...] = jnp.zeros_like(yo)
    ssq[...] = jnp.zeros_like(ssq)
    loads[2].wait()

    def project(t):
        block = xbuf[t].astype(F32)
        ssq[...] += jnp.sum(block * block, axis=-1, keepdims=True)
        scaled = (block * gain_ref[pl.ds(t, 1), :]).astype(BF16)
        part = pl.ds(pl.multiple_of(t * chunk, 64), chunk)
        yq[...] += dot(scaled, qw[part, :])
        yo[...] += dot(scaled, wo[part, :])

    project(tp)
    for copy in first:
        copy.wait_send()
        started.remove(copy)
    for n, i in enumerate((1, 2, 0)):
        zo = z_others[i]
        cols = pl.ds(pl.multiple_of(zo * 128, 128), 128)
        device = at(grp, zo * 4 + s)
        for n2, (src, dst) in enumerate(
            ((k_hbm.at[:, :, cols], kbuf), (v_hbm.at[:, :, cols], vbuf), (dbuf.at[z], dbuf))
        ):
            started.append(
                send(src, dst.at[z], kv_send.at[i * 3 + n2], kv_recv.at[z * 3 + n2], device)
            )
    for i, zo in enumerate(z_others):
        t = zo * 4 + s
        arrive(xbuf.at[t], x_send.at[0], x_recv.at[t])
        send_x(t, 4 + i, across)
        send_x(t, 8 + i, sibling)
        project(t)
    for i, zo in enumerate([z] + z_others):
        t = zo * 4 + (1 - y) * 2 + c
        arrive(xbuf.at[t], x_send.at[0], x_recv.at[t])
        send_x(t, 11 + i, sibling)
        project(t)
    for zo in [z] + z_others:
        for yo_ in (y, 1 - y):
            t = zo * 4 + yo_ * 2 + (1 - c)
            arrive(xbuf.at[t], x_send.at[0], x_recv.at[t])
            project(t)

    rinv = lax.rsqrt(ssq[...] * (1.0 / width) + 1e-06)
    other = yo[...] * rinv
    low = other[:, 64:128].astype(BF16)
    adapter = adapter_ref[...]
    wide = lanes((rows, 256))
    picked = (wide // 16) == adapter
    row_of = lax.broadcasted_iota(jnp.int32, (64, 256), 0)
    col_of = lanes((64, 256)) % 16

    def spread(part, offset):
        tile = (row_of == col_of + offset).astype(F32).astype(BF16)
        return jnp.where(picked, dot(part, tile), 0.0).astype(BF16)

    queries = (yq[...] * rinv + dot(spread(low, 0), qu_ref[...].reshape(256, 256))).astype(BF16)
    odd = tp % 2
    is_key = tp < 8
    kv_low = jnp.where(is_key, spread(low, 16).astype(F32), spread(low, 32).astype(F32)).astype(BF16)
    pair_cols = pl.ds(pl.multiple_of((tp // 2) * 128, 128), 128)
    kv_update = dot(kv_low, ku_ref[:, :, pair_cols].reshape(256, 128))
    kv_base = other[:, :64]
    kv_full = jnp.concatenate([kv_base, kv_base], axis=1) + kv_update
    narrow = lanes((rows, 128))
    fresh[...] = jnp.where((narrow // 64) == odd, kv_full, 0.0).astype(BF16)
    fold_row = lax.broadcasted_iota(jnp.int32, (256, 128), 0) % 16
    fold_col = lanes((256, 128))
    key_up = ku_ref[:, :, pl.ds(pl.multiple_of(z * 128, 128), 128)].reshape(256, 128)
    factors = jnp.zeros((rows, 128), F32)
    for h in range(2):
        full = dot_nt(queries[:, h * 128 : (h + 1) * 128], key_up)
        full = jnp.where(picked, full, 0.0).astype(BF16)
        fold = (fold_col == fold_row + 16 * h).astype(F32).astype(BF16)
        factors = factors + dot(full, fold)
    mine = 4 * grp + s
    qbuf[mine, :, :256] = queries
    qbuf[mine, :, 256:] = factors.astype(BF16)

    n = 0
    for g, shift in ((1 - grp, 0), (1 - grp, 1), (1 - grp, 2), (1 - grp, 3), (grp, 1), (grp, 2), (grp, 3)):
        device = at(g, z * 4 + (s + shift) % 4)
        started.append(send(qbuf.at[mine], qbuf.at[mine], q_send.at[n], q_recv.at[mine], device))
        n += 1
    head = (tp % 8) // 2
    slot = (tp // 8) * 2 + odd
    for j in range(4):
        target = head * 4 + j

        @pl.when(target != tp)
        def _():
            send(fresh, fresh_in.at[slot], f_send.at[j], f_recv.at[slot], at(grp, target))

        @pl.when(target == tp)
        def _():
            fresh_in[slot] = fresh[...]

    def augment(zo):
        for p in range(4):
            part = pl.ds(p * 128, 128)
            down = dbuf[zo, :, p * 32 : (p + 1) * 32]
            kaug[part, :128] = kbuf[zo, p]
            kaug[part, 128:] = jnp.concatenate(
                [down[:, :16], down[:, :16], jnp.zeros((128, 96), BF16)], axis=1
            )
            right = jnp.concatenate([down[:, 16:], jnp.zeros((128, 112), BF16)], axis=1)
            vaug[part, :128] = vbuf[zo, p]
            vaug[part, 128:] = jnp.where(
                lanes((128, 128)) == 16, 1.0, right.astype(F32)
            ).astype(BF16)

    def attend(j, start):
        scores = dot_nt(lhs[j], kaug[...]) * scale
        top = jnp.max(scores, axis=-1, keepdims=True)
        if not start:
            old = peak[j]
            top = jnp.maximum(old, top)
        weights = jnp.exp2(scores - top).astype(BF16)
        product = dot(weights, vaug[...])
        if start:
            acc[j] = product
        else:
            acc[j] = acc[j] * jnp.exp2(old - top) + product
        peak[j] = top

    loads[3].wait()
    loads[4].wait()
    augment(z)
    f_lane = lanes((rows, 128)) // 16
    for shift in range(4):
        j = (s + shift) % 4
        for g, local in ((grp, True), (1 - grp, False)):
            index = 4 * g + j
            if not (local and shift == 0):
                arrive(qbuf.at[index], x_send.at[0], q_recv.at[index])
            extra = qbuf[index, :, 256:].astype(F32)
            for h in range(2):
                part = pl.ds(pl.multiple_of(h * 256 + g * 128, 128), 128)
                lhs[j, part, :128] = qbuf[index, :, h * 128 : (h + 1) * 128]
                lhs[j, part, 128:] = jnp.where(f_lane == h, extra, 0.0).astype(BF16)
        attend(j, True)

    def arrived(zo):
        for n2, dst in enumerate((kbuf, vbuf, dbuf)):
            arrive(dst.at[zo], x_send.at[0], kv_recv.at[zo * 3 + n2])

    for zo in z_others[:2]:
        arrived(zo)
        augment(zo)

        def body(j, carry):
            attend(j, False)
            return carry

        lax.fori_loop(0, 4, body, 0)

    arrived(z_others[2])
    augment(z_others[2])

    def last(shift, carry):
        j = (s + shift) % 4
        attend(j, False)
        lane = lanes((128, 128))
        for g in range(2):
            stats = None
            for h in range(2):
                part = pl.ds(h * 256 + g * 128, 128)
                psend[j, g, :, h * 128 : (h + 1) * 128] = acc[j, part, :128].astype(BF16)
                tail = acc[j, part, 128:]
                high = tail.astype(BF16).astype(F32)
                m0, m1, m2 = split_three(peak[j, part, :])
                one = high + pltpu.roll(tail - high, 32, 1)
                one = jnp.where(lane == 24, m0, one)
                one = jnp.where(lane == 25, m1, one)
                one = jnp.where(lane == 26, m2, one)
                stats = one if h == 0 else stats + pltpu.roll(one, 64, 1)
            psend[j, g, :, 256:] = stats.astype(BF16)
            here = jnp.logical_and(j == s, grp == g)

            @pl.when(jnp.logical_not(here))
            def _():
                send(psend.at[j, g], pbuf.at[mine], p_send.at[j * 2 + g], p_recv.at[mine], at(g, z * 4 + j))

            @pl.when(here)
            def _():
                pbuf[mine] = psend[j, g]

        return carry

    lax.fori_loop(1, 5, last, 0)

    for n in range(4):
        source = (n // 2) * 8 + 2 * z + n % 2

        @pl.when(source != tp)
        def _():
            arrive(fresh_in.at[n], x_send.at[0], f_recv.at[n])

    own_key = fresh_in[0].astype(F32) + fresh_in[1].astype(F32)
    own_value = fresh_in[2].astype(F32) + fresh_in[3].astype(F32)
    for n in range(1, 8):
        index = (mine + n) % 8
        arrive(pbuf.at[index], x_send.at[0], p_recv.at[index])
    half = slots_ref.shape[1]
    document = doc_ref[...]
    holder = jnp.where(document == 0, slots_ref[0, 0] // half, slots_ref[1, 0] // half)
    narrow = lanes((rows, 128))
    picked = (lanes((rows, 256)) // 16) == adapter_ref[...]
    value_up = ku_ref[:, :, pl.ds(pl.multiple_of(512 + z * 128, 128), 128)].reshape(256, 128)
    row_of = lax.broadcasted_iota(jnp.int32, (128, 256), 0)
    tile = (row_of == lanes((128, 256)) % 16).astype(F32).astype(BF16)
    blocks = [
        jnp.where(holder == 0, pbuf[j].astype(F32), pbuf[4 + j].astype(F32)) for j in range(4)
    ]
    for h in range(2):
        query = qbuf[mine, :, h * 128 : (h + 1) * 128].astype(F32)
        own = jnp.sum(query * own_key, axis=-1, keepdims=True) * scale
        top = own
        parts = []
        for block in blocks:
            stats = block[:, 256:]
            if h:
                stats = pltpu.roll(stats, 64, 1)
            at_peak = jnp.logical_and(narrow >= 24, narrow < 27)
            m = jnp.sum(jnp.where(at_peak, stats, 0.0), axis=-1, keepdims=True)
            tail = jnp.where(narrow < 17, stats + pltpu.roll(stats, 96, 1), 0.0)
            top = jnp.maximum(top, m)
            parts.append((block[:, h * 128 : (h + 1) * 128], tail, m))
        own_weight = jnp.exp2(own - top)
        numerator = own_weight * own_value
        tail_sum = jnp.zeros((rows, 128), F32)
        for num, tail, m in parts:
            weight = jnp.exp2(m - top)
            numerator = numerator + num * weight
            tail_sum = tail_sum + tail * weight
        total = jnp.sum(jnp.where(narrow == 16, tail_sum, 0.0), axis=-1, keepdims=True) + own_weight
        factor = jnp.where(narrow < 16, tail_sum, 0.0)
        high = factor.astype(BF16)
        shift = jnp.zeros((rows, 128), F32)
        for piece in (high, (factor - high.astype(F32)).astype(BF16)):
            expanded = jnp.where(picked, dot(piece, tile), 0.0).astype(BF16)
            shift = shift + dot(expanded, value_up)
        out_ref[:, h * 128 : (h + 1) * 128] = ((numerator + shift) / total).astype(BF16)

    for copy in started:
        copy.wait_send()
    for j in range(4):
        target = head * 4 + j

        @pl.when(target != tp)
        def _():
            pltpu.make_async_remote_copy(
                src_ref=fresh, dst_ref=fresh_in.at[slot], send_sem=f_send.at[j],
                recv_sem=f_recv.at[slot], device_id=at(grp, target), device_id_type=MESH,
            ).wait_send()

    for j in range(4):
        for g in range(2):

            @pl.when(jnp.logical_not(jnp.logical_and(j == s, grp == g)))
            def _():
                pltpu.make_async_remote_copy(
                    src_ref=psend.at[j, g], dst_ref=pbuf.at[mine], send_sem=p_send.at[j * 2 + g],
                    recv_sem=p_recv.at[mine], device_id=at(g, z * 4 + j), device_id_type=MESH,
                ).wait_send()


def fused_device(
    residual_input, input_norm_gain, query_weight, key_value_weight, shared_down_factors,
    query_up_factors, key_value_up_factors, paged_base_keys, paged_base_values,
    paged_down_factors, adapter_of_row, document_of_row, document_page_slots,
):
    rows, chunk = residual_input.shape
    vmem = pl.BlockSpec(memory_space=pltpu.VMEM)
    hbm = pl.BlockSpec(memory_space=pl.ANY)
    smem = pl.BlockSpec(memory_space=pltpu.SMEM)
    dma = pltpu.SemaphoreType.DMA
    width = 16 * chunk
    return pl.pallas_call(
        fused_kernel,
        out_shape=jax.ShapeDtypeStruct((rows, 256), BF16),
        in_specs=[vmem, vmem, hbm, hbm, hbm, vmem, vmem, hbm, hbm, vmem, vmem, vmem, smem],
        out_specs=vmem,
        scratch_shapes=[
            pltpu.VMEM((16, rows, chunk), BF16),
            pltpu.VMEM((width, 256), BF16),
            pltpu.VMEM((width, 64), BF16),
            pltpu.VMEM((width, 48), BF16),
            pltpu.VMEM((width, 128), BF16),
            pltpu.VMEM((rows, 256), F32),
            pltpu.VMEM((rows, 128), F32),
            pltpu.VMEM((rows, 1), F32),
            pltpu.VMEM((4, 4, 128, 128), BF16),
            pltpu.VMEM((4, 4, 128, 128), BF16),
            pltpu.VMEM((4, 128, 128), BF16),
            pltpu.VMEM((8, rows, 384), BF16),
            pltpu.VMEM((4, 4 * rows, 256), BF16),
            pltpu.VMEM((512, 256), BF16),
            pltpu.VMEM((512, 256), BF16),
            pltpu.VMEM((4, 4 * rows, 256), F32),
            pltpu.VMEM((4, 4 * rows, 1), F32),
            pltpu.VMEM((4, 2, rows, 384), BF16),
            pltpu.VMEM((8, rows, 384), BF16),
            pltpu.VMEM((rows, 128), BF16),
            pltpu.VMEM((4, rows, 128), BF16),
            dma((5,)), dma((16,)), dma((16,)), dma((9,)), dma((12,)),
            dma((7,)), dma((8,)), dma((4,)), dma((4,)), dma((8,)), dma((8,)),
        ],
        compiler_params=pltpu.CompilerParams(
            collective_id=0, has_side_effects=True, vmem_limit_bytes=48 * 1024 * 1024
        ),
        cost_estimate=pl.CostEstimate(
            flops=5_000_000_000, bytes_accessed=8_000_000, transcendentals=4_500_000
        ),
    )(
        residual_input, input_norm_gain.reshape(16, chunk), query_weight, key_value_weight,
        shared_down_factors, query_up_factors, key_value_up_factors, paged_base_keys,
        paged_base_values, paged_down_factors, adapter_of_row.reshape(rows, 1),
        document_of_row, document_page_slots,
    )


def merge_slices(numerator, factor_sum, maxima, totals):
    peak_all = jnp.max(maxima, axis=-1)
    weight = jnp.exp(maxima - peak_all[..., None])
    numerator = jnp.sum(numerator * weight[..., None], axis=-2)
    factor_sum = jnp.sum(factor_sum * weight[..., None], axis=-2)
    totals = jnp.sum(totals * weight, axis=-1)
    return (numerator, factor_sum, peak_all, totals)


def attend_local(
    query_matrix,
    down_factors,
    paged_base_keys,
    paged_base_values,
    paged_down_factors,
    heads_kv,
    low_rank_width,
):
    item_count = query_matrix.shape[0]
    head_size = paged_base_keys.shape[-1] // heads_kv
    all_heads = query_matrix.shape[1] // head_size
    query_group_size = all_heads // heads_kv
    local_tokens = paged_base_keys.shape[0] * paged_base_keys.shape[1]
    score_scaling = head_size ** (-0.5)
    key_heads = paged_base_keys.reshape(local_tokens, heads_kv, head_size).transpose(1, 0, 2)
    value_heads = paged_base_values.reshape(local_tokens, heads_kv, head_size).transpose(1, 0, 2)
    factor_flat = paged_down_factors.reshape(local_tokens, 2 * low_rank_width)
    cached_key = factor_flat[:, :low_rank_width]
    cached_value = factor_flat[:, low_rank_width:]
    query_head_count = query_matrix.reshape(
        item_count, heads_kv, query_group_size, head_size
    ).transpose(1, 0, 2, 3)
    factor_heads = down_factors.reshape(
        item_count, heads_kv, query_group_size, low_rank_width
    ).transpose(1, 0, 2, 3)

    def one_head(bundle):
        query_one, factor_one, key_one, value_one = bundle
        scores = (
            jnp.einsum("ngd,ld->ngl", query_one, key_one, preferred_element_type=jnp.float32)
            + jnp.einsum("ngj,lj->ngl", factor_one, cached_key, preferred_element_type=jnp.float32)
        ) * score_scaling
        maxima = jnp.max(scores, -1)
        weights = jnp.exp(scores - maxima[..., None])
        totals = jnp.sum(weights, -1)
        rounded = weights.astype(jnp.bfloat16)
        numerator = jnp.einsum(
            "ngl,ld->ngd", rounded, value_one, preferred_element_type=jnp.float32
        )
        factor_sum = jnp.einsum(
            "ngl,lj->ngj", rounded, cached_value, preferred_element_type=jnp.float32
        )
        return (numerator, factor_sum, maxima, totals)

    numerator, factor_sum, maxima, totals = lax.map(
        one_head, (query_head_count, factor_heads, key_heads, value_heads)
    )
    numerator = numerator.transpose(1, 0, 2, 3).reshape(item_count, all_heads, head_size)
    factor_sum = factor_sum.transpose(1, 0, 2, 3).reshape(item_count, all_heads, low_rank_width)
    maxima = maxima.transpose(1, 0, 2).reshape(item_count, all_heads)
    totals = totals.transpose(1, 0, 2).reshape(item_count, all_heads)
    return (numerator, factor_sum, maxima, totals)


def per_device(
    residual_input,
    input_norm_gain,
    query_weight,
    key_value_weight,
    shared_down_factors,
    query_up_factors,
    key_value_up_factors,
    paged_base_keys,
    paged_base_values,
    paged_down_factors,
    adapter_of_row,
    document_of_row,
    document_page_slots,
):
    tp_count = lax.axis_size("tp")
    grp_count = lax.axis_size("grp")
    tp_index = lax.axis_index("tp")
    low_rank_width = shared_down_factors.shape[1] // 3
    key_value_width = key_value_up_factors.shape[2] // 2
    head_size = HEAD_SIZE
    heads_kv = key_value_width // head_size
    row_count = residual_input.shape[0]
    score_scaling = head_size ** (-0.5)
    gathered = lax.all_gather(residual_input, "tp", axis=1, tiled=True).astype(jnp.float32)
    normed_input = (
        gathered
        * lax.rsqrt(jnp.mean(gathered * gathered, -1, keepdims=True) + 1e-06)
        * input_norm_gain
    ).astype(jnp.bfloat16)
    low_rank_part = jnp.dot(
        normed_input, shared_down_factors, preferred_element_type=jnp.float32
    ).astype(jnp.bfloat16)
    query_low_rank = low_rank_part[:, :low_rank_width]
    key_low_rank = low_rank_part[:, low_rank_width : 2 * low_rank_width]
    value_low_rank = low_rank_part[:, 2 * low_rank_width :]
    query_update = query_up_factors[adapter_of_row]
    query_part = (
        jnp.dot(normed_input, query_weight, preferred_element_type=jnp.float32)
        + jnp.einsum("ep,epg->eg", query_low_rank, query_update, preferred_element_type=jnp.float32)
    ).astype(jnp.bfloat16)
    key_value_columns = key_value_weight.shape[1]
    key_value_start = tp_index * key_value_columns
    key_value_update = lax.dynamic_slice_in_dim(
        key_value_up_factors, key_value_start, key_value_columns, 2
    )[adapter_of_row]
    key_value_low = jnp.where(key_value_start < key_value_width, key_low_rank, value_low_rank)
    kv_part = (
        jnp.dot(normed_input, key_value_weight, preferred_element_type=jnp.float32)
        + jnp.einsum(
            "ep,epg->eg", key_value_low, key_value_update, preferred_element_type=jnp.float32
        )
    ).astype(jnp.bfloat16)
    heads_here = query_part.shape[1] // head_size
    query_group_size = heads_here * tp_count // heads_kv
    key_value_head = tp_index * heads_here // query_group_size
    key_column_count = lax.dynamic_slice_in_dim(
        key_value_up_factors, key_value_head * head_size, head_size, 2
    )[adapter_of_row]
    my_queries = query_part.reshape(row_count, heads_here, head_size)
    factor_part = jnp.einsum(
        "rhd,rjd->rhj", my_queries, key_column_count, preferred_element_type=jnp.float32
    ).astype(jnp.bfloat16)
    factor_part = factor_part.reshape(row_count, heads_here * low_rank_width)
    query_matrix, down_factors, fresh_kv = (
        lax.all_gather(query_part, "tp", axis=1, tiled=True),
        lax.all_gather(factor_part, "tp", axis=1, tiled=True),
        lax.all_gather(kv_part, "tp", axis=1, tiled=True),
    )
    doc_pages = document_page_slots.shape[1]
    owner_of_doc = document_page_slots[:, 0] // doc_pages
    doc_ids = document_of_row[:, 0]
    doc_match = (doc_ids[:, None] == jnp.arange(document_page_slots.shape[0])[None, :]).astype(
        jnp.int32
    )
    target = jnp.sum(doc_match * owner_of_doc[None, :], 1)
    target_match = (target[:, None] == jnp.arange(grp_count)[None, :]).astype(jnp.int32)
    earlier = jnp.cumsum(target_match, 0) - target_match
    capacity = 2 * row_count // grp_count
    slot_of = target * capacity + jnp.sum(earlier * target_match, 1)
    placing = (jnp.arange(grp_count * capacity)[:, None] == slot_of[None, :]).astype(jnp.bfloat16)
    send_queries = (
        jnp.dot(placing, query_matrix, preferred_element_type=jnp.float32)
        .astype(jnp.bfloat16)
        .reshape(grp_count, capacity, -1)
    )
    send_factors = (
        jnp.dot(placing, down_factors, preferred_element_type=jnp.float32)
        .astype(jnp.bfloat16)
        .reshape(grp_count, capacity, -1)
    )
    query_in = lax.all_to_all(send_queries, "grp", split_axis=0, concat_axis=0, tiled=True)
    factor_in = lax.all_to_all(send_factors, "grp", split_axis=0, concat_axis=0, tiled=True)
    per_source = query_in.shape[1]
    item_count = query_in.shape[0] * per_source
    query_flat = query_in.reshape(item_count, -1)
    factor_flat = factor_in.reshape(item_count, -1)
    numerator, factor_sum, maxima, totals = attend_local(
        query_flat,
        factor_flat,
        paged_base_keys,
        paged_base_values,
        paged_down_factors,
        heads_kv,
        low_rank_width,
    )
    all_heads = numerator.shape[1]
    returned = (
        lax.all_to_all(
            numerator.reshape(grp_count, per_source, all_heads, head_size),
            "grp",
            split_axis=0,
            concat_axis=0,
            tiled=True,
        ),
        lax.all_to_all(
            factor_sum.reshape(grp_count, per_source, all_heads, low_rank_width),
            "grp",
            split_axis=0,
            concat_axis=0,
            tiled=True,
        ),
        lax.all_to_all(
            maxima.reshape(grp_count, per_source, all_heads),
            "grp",
            split_axis=0,
            concat_axis=0,
            tiled=True,
        ),
        lax.all_to_all(
            totals.reshape(grp_count, per_source, all_heads),
            "grp",
            split_axis=0,
            concat_axis=0,
            tiled=True,
        ),
    )
    numerator, factor_sum, maxima, totals = [
        piece.reshape((grp_count * capacity,) + piece.shape[2:])[slot_of] for piece in returned
    ]
    numerator, factor_sum, maxima, totals = (
        lax.all_to_all(numerator[:, :, None, :], "tp", split_axis=1, concat_axis=2, tiled=True),
        lax.all_to_all(factor_sum[:, :, None, :], "tp", split_axis=1, concat_axis=2, tiled=True),
        lax.all_to_all(maxima[:, :, None], "tp", split_axis=1, concat_axis=2, tiled=True),
        lax.all_to_all(totals[:, :, None], "tp", split_axis=1, concat_axis=2, tiled=True),
    )
    numerator, factor_sum, maxima, totals = merge_slices(numerator, factor_sum, maxima, totals)
    own_key = lax.dynamic_slice_in_dim(fresh_kv, key_value_head * head_size, head_size, 1)
    value_own = lax.dynamic_slice_in_dim(
        fresh_kv, key_value_width + key_value_head * head_size, head_size, 1
    )
    own_token_score = (
        jnp.einsum("rhd,rd->rh", my_queries, own_key, preferred_element_type=jnp.float32)
        * score_scaling
    )
    peak_all = jnp.maximum(maxima, own_token_score)
    old_scale = jnp.exp(maxima - peak_all)
    own_weight = jnp.exp(own_token_score - peak_all)
    numerator = (
        numerator * old_scale[..., None]
        + own_weight[..., None] * value_own.astype(jnp.float32)[:, None, :]
    )
    factor_sum = factor_sum * old_scale[..., None]
    totals = totals * old_scale + own_weight
    value_column_count = lax.dynamic_slice_in_dim(
        key_value_up_factors, key_value_width + key_value_head * head_size, head_size, 2
    )[adapter_of_row]
    value_shift = jnp.einsum(
        "rhj,rjd->rhd",
        factor_sum,
        value_column_count.astype(jnp.float32),
        precision=lax.Precision.HIGHEST,
    )
    result = ((numerator + value_shift) / totals[..., None]).astype(jnp.bfloat16)
    return result.reshape(row_count, heads_here * head_size)


def solution(mesh):
    in_specs = (
        P("grp", "tp"),
        P(),
        P(None, "tp"),
        P(None, "tp"),
        P(),
        P(None, None, "tp"),
        P(),
        P(("grp", "tp"), None, None),
        P(("grp", "tp"), None, None),
        P(("grp", "tp"), None, None),
        P("grp"),
        P("grp", None),
        P(),
    )
    out_specs = P("grp", "tp")
    fits = mesh.shape["grp"] == 2 and mesh.shape["tp"] == 16
    return jax.shard_map(
        fused_device if fits else per_device, mesh=mesh, in_specs=in_specs, out_specs=out_specs, check_vma=False
    )
```

```python
import functools
import math

import jax
import jax.numpy as jnp
from jax import lax
from jax.experimental import pallas as pl
from jax.experimental.pallas import tpu as pltpu
from jax.sharding import PartitionSpec as P

HEAD_SIZE = 128
MESH = pl.DeviceIdType.MESH
F32 = jnp.float32
BF16 = jnp.bfloat16


def dot(a, b):
    return jnp.dot(a, b, preferred_element_type=F32)


def dot_nt(a, b):
    return lax.dot_general(a, b, (((1,), (1,)), ((), ())), preferred_element_type=F32)


def lanes(shape):
    return lax.broadcasted_iota(jnp.int32, shape, len(shape) - 1)


def split_three(value):
    high = value.astype(BF16).astype(F32)
    middle = (value - high).astype(BF16).astype(F32)
    low = (value - high - middle).astype(BF16).astype(F32)
    return high, middle, low


def fused_kernel(
    x_ref, gain_ref, qw_hbm, kvw_hbm, dn_hbm, qu_hbm, ku_hbm, k_hbm, v_hbm, d_ref,
    adapter_ref, doc_ref, slots_ref, out_ref,
    xbuf, qw, kvw, dn, qu_ref, ku_ref, wo, yq, yo, ssq, kbuf, vbuf, dbuf, qbuf, lhs, kaug, vaug,
    acc, peak, psend, pbuf, fresh, fresh_in,
    load_sem, x_send, x_recv, kv_send, kv_recv, q_send, q_recv, f_send, f_recv, p_send, p_recv,
):
    chunk, rows = x_ref.shape
    width = 16 * chunk
    grp = lax.axis_index("grp")
    tp = lax.axis_index("tp")
    z = tp // 4
    s = tp % 4
    y = s // 2
    c = s % 2
    scale = math.log2(math.e) / math.sqrt(HEAD_SIZE)

    def at(g, t):
        return {"grp": g, "tp": t}

    sibling = at(grp, z * 4 + y * 2 + (1 - c))
    across = at(grp, z * 4 + (1 - y) * 2 + c)
    z_others = [z + 1 - 2 * (z % 2), (z + 2) % 4, 3 - z]

    loads = [
        pltpu.make_async_copy(src, dst, load_sem.at[i])
        for i, (src, dst) in enumerate(
            ((kvw_hbm, kvw), (dn_hbm, dn), (qw_hbm, qw),
             (k_hbm.at[:, :, pl.ds(pl.multiple_of(z * 128, 128), 128)], kbuf.at[z]),
             (v_hbm.at[:, :, pl.ds(pl.multiple_of(z * 128, 128), 128)], vbuf.at[z]),
             (qu_hbm, qu_ref), (ku_hbm, ku_ref))
        )
    ]
    for load in loads:
        load.start()

    barrier = pltpu.get_barrier_semaphore()
    for i in range(1, 16):
        pl.semaphore_signal(barrier, inc=1, device_id=at(grp, (tp + i) % 16), device_id_type=MESH)
    for j in range(4):
        pl.semaphore_signal(barrier, inc=1, device_id=at(1 - grp, z * 4 + j), device_id_type=MESH)
    dbuf[z] = d_ref[...].reshape(128, 128).T
    gain = jnp.zeros((1, chunk), F32)
    for t in range(16):
        gain = gain + jnp.where(tp == t, gain_ref[:, t * chunk : (t + 1) * chunk], 0.0)
    x_rows = x_ref[...].T.astype(F32)
    pieces = split_three(jnp.sum(x_rows * x_rows, axis=-1, keepdims=True))
    xbuf[tp, :, :chunk] = (x_rows * gain).astype(BF16)
    spare = lanes((rows, 384 - chunk))
    sums = jnp.zeros(spare.shape, F32)
    for i, piece in enumerate(pieces):
        sums = jnp.where(spare == i, piece, sums)
    xbuf[tp, :, chunk:] = sums.astype(BF16)
    pl.semaphore_wait(barrier, 19)

    started = []

    def send(src, dst, send_sem, recv_sem, device):
        copy = pltpu.make_async_remote_copy(
            src_ref=src, dst_ref=dst, send_sem=send_sem, recv_sem=recv_sem,
            device_id=device, device_id_type=MESH,
        )
        copy.start()
        return copy

    def arrive(dst, send_sem, recv_sem):
        pltpu.make_async_remote_copy(
            src_ref=dst, dst_ref=dst, send_sem=send_sem, recv_sem=recv_sem,
            device_id=sibling, device_id_type=MESH,
        ).wait_recv()

    def send_x(t, sem, device):
        copy = send(xbuf.at[t], xbuf.at[t], x_send.at[sem], x_recv.at[t], device)
        started.append(copy)
        return copy

    send_x(tp, 0, at(grp, z_others[1] * 4 + s))
    send_x(tp, 1, at(grp, z_others[0] * 4 + s))
    send_x(tp, 3, across)
    send_x(tp, 7, sibling)
    for i in (1, 2, 0):
        zo = z_others[i]
        cols = pl.ds(pl.multiple_of(zo * 128, 128), 128)
        device = at(grp, zo * 4 + s)
        for n2, (src, dst) in enumerate(
            ((k_hbm.at[:, :, cols], kbuf), (v_hbm.at[:, :, cols], vbuf), (dbuf.at[z], dbuf))
        ):
            started.append(
                send(src, dst.at[z], kv_send.at[i * 3 + n2], kv_recv.at[z * 3 + n2], device)
            )

    loads[0].wait()
    loads[1].wait()

    def join(i, carry):
        part = pl.ds(pl.multiple_of(i * 128, 128), 128)
        both = jnp.concatenate([kvw[:, part], dn[:, part], jnp.zeros((16, 128), BF16)], axis=0)
        wo[part, :] = both.T
        return carry

    lax.fori_loop(0, width // 128, join, 0)
    yq[...] = jnp.zeros_like(yq)
    yo[...] = jnp.zeros_like(yo)
    ssq[...] = jnp.zeros_like(ssq)
    loads[2].wait()

    def project(t):
        scaled = xbuf[t, :, :chunk]
        ssq[...] += jnp.sum(xbuf[t, :, chunk:].astype(F32), axis=-1, keepdims=True)
        part = pl.ds(pl.multiple_of(t * chunk, 64), chunk)
        yq[...] += dot(scaled, qw[part, :])
        yo[...] += dot(scaled, wo[part, :])

    project(tp)
    for i in (1, 0, 2):
        t = z_others[i] * 4 + s
        arrive(xbuf.at[t], x_send.at[0], x_recv.at[t])
        if i == 1:
            send_x(t, 2, at(grp, z_others[0] * 4 + s))
        send_x(t, 4 + i, across)
        send_x(t, 8 + i, sibling)
        project(t)
    for i, zo in enumerate([z] + z_others):
        t = zo * 4 + (1 - y) * 2 + c
        arrive(xbuf.at[t], x_send.at[0], x_recv.at[t])
        send_x(t, 11 + i, sibling)
        project(t)
    for zo in [z] + z_others:
        for yo_ in (y, 1 - y):
            t = zo * 4 + yo_ * 2 + (1 - c)
            arrive(xbuf.at[t], x_send.at[0], x_recv.at[t])
            project(t)

    rinv = lax.rsqrt(ssq[...] * (1.0 / width) + 1e-06)
    other = yo[...] * rinv
    low = other[:, 64:128].astype(BF16)
    def column(row_ref):
        return jnp.broadcast_to(row_ref[...].astype(F32), (rows, rows)).T.astype(jnp.int32)

    adapter = column(adapter_ref)
    adapter = jnp.concatenate([adapter, adapter], axis=1)
    loads[5].wait()
    loads[6].wait()
    wide = lanes((rows, 256))
    picked = (wide // 16) == adapter
    row_of = lax.broadcasted_iota(jnp.int32, (64, 256), 0)
    col_of = lanes((64, 256)) % 16

    def spread(part, offset):
        tile = (row_of == col_of + offset).astype(F32).astype(BF16)
        return jnp.where(picked, dot(part, tile), 0.0).astype(BF16)

    queries = (yq[...] * rinv + dot(spread(low, 0), qu_ref[...].reshape(256, 256))).astype(BF16)
    odd = tp % 2
    is_key = tp < 8
    kv_low = jnp.where(is_key, spread(low, 16).astype(F32), spread(low, 32).astype(F32)).astype(BF16)
    pair_cols = pl.ds(pl.multiple_of((tp // 2) * 128, 128), 128)
    kv_update = dot(kv_low, ku_ref[:, :, pair_cols].reshape(256, 128))
    kv_base = other[:, :64]
    kv_full = jnp.concatenate([kv_base, kv_base], axis=1) + kv_update
    narrow = lanes((rows, 128))
    fresh[...] = jnp.where((narrow // 64) == odd, kv_full, 0.0).astype(BF16)
    fold_row = lax.broadcasted_iota(jnp.int32, (256, 128), 0) % 16
    fold_col = lanes((256, 128))
    key_up = ku_ref[:, :, pl.ds(pl.multiple_of(z * 128, 128), 128)].reshape(256, 128)
    factors = jnp.zeros((rows, 128), F32)
    for h in range(2):
        full = dot_nt(queries[:, h * 128 : (h + 1) * 128], key_up)
        full = jnp.where(picked, full, 0.0).astype(BF16)
        fold = (fold_col == fold_row + 16 * h).astype(F32).astype(BF16)
        factors = factors + dot(full, fold)
    mine = 4 * grp + s
    qbuf[mine, :, :256] = queries
    qbuf[mine, :, 256:] = factors.astype(BF16)

    n = 0
    for g, shift in ((1 - grp, 0), (1 - grp, 1), (1 - grp, 2), (1 - grp, 3), (grp, 1), (grp, 2), (grp, 3)):
        device = at(g, z * 4 + (s + shift) % 4)
        started.append(send(qbuf.at[mine], qbuf.at[mine], q_send.at[n], q_recv.at[mine], device))
        n += 1
    head = (tp % 8) // 2
    slot = (tp // 8) * 2 + odd
    for j in range(4):
        target = head * 4 + j

        @pl.when(target != tp)
        def _():
            send(fresh, fresh_in.at[slot], f_send.at[j], f_recv.at[slot], at(grp, target))

        @pl.when(target == tp)
        def _():
            fresh_in[slot] = fresh[...]

    def augment(zo):
        for p in range(4):
            part = pl.ds(p * 128, 128)
            down = dbuf[zo, :, p * 32 : (p + 1) * 32]
            kaug[part, :128] = kbuf[zo, p]
            kaug[part, 128:] = jnp.concatenate(
                [down[:, :16], down[:, :16], jnp.zeros((128, 96), BF16)], axis=1
            )
            right = jnp.concatenate([down[:, 16:], jnp.zeros((128, 112), BF16)], axis=1)
            vaug[part, :128] = vbuf[zo, p]
            vaug[part, 128:] = jnp.where(
                lanes((128, 128)) == 16, 1.0, right.astype(F32)
            ).astype(BF16)

    def attend(j, start):
        scores = dot_nt(lhs[j], kaug[...]) * scale
        top = jnp.max(scores, axis=-1, keepdims=True)
        if not start:
            old = peak[j]
            top = jnp.maximum(old, top)
        weights = jnp.exp2(scores - top).astype(BF16)
        product = dot(weights, vaug[...])
        if start:
            acc[j] = product
        else:
            acc[j] = acc[j] * jnp.exp2(old - top) + product
        peak[j] = top

    loads[3].wait()
    loads[4].wait()
    augment(z)
    f_lane = lanes((rows, 128)) // 16
    for shift in range(4):
        j = (s + shift) % 4
        for g, local in ((grp, True), (1 - grp, False)):
            index = 4 * g + j
            if not (local and shift == 0):
                arrive(qbuf.at[index], x_send.at[0], q_recv.at[index])
            extra = qbuf[index, :, 256:].astype(F32)
            for h in range(2):
                part = pl.ds(pl.multiple_of(h * 256 + g * 128, 128), 128)
                lhs[j, part, :128] = qbuf[index, :, h * 128 : (h + 1) * 128]
                lhs[j, part, 128:] = jnp.where(f_lane == h, extra, 0.0).astype(BF16)
        attend(j, True)

    def arrived(zo):
        for n2, dst in enumerate((kbuf, vbuf, dbuf)):
            arrive(dst.at[zo], x_send.at[0], kv_recv.at[zo * 3 + n2])

    for zo in z_others[:2]:
        arrived(zo)
        augment(zo)

        def body(j, carry):
            attend(j, False)
            return carry

        lax.fori_loop(0, 4, body, 0)

    arrived(z_others[2])
    augment(z_others[2])

    def last(shift, carry):
        j = (s + shift) % 4
        attend(j, False)
        lane = lanes((128, 128))
        for g in range(2):
            stats = None
            for h in range(2):
                part = pl.ds(h * 256 + g * 128, 128)
                psend[j, g, :, h * 128 : (h + 1) * 128] = acc[j, part, :128].astype(BF16)
                tail = acc[j, part, 128:]
                high = tail.astype(BF16).astype(F32)
                m0, m1, m2 = split_three(peak[j, part, :])
                one = high + pltpu.roll(tail - high, 32, 1)
                one = jnp.where(lane == 24, m0, one)
                one = jnp.where(lane == 25, m1, one)
                one = jnp.where(lane == 26, m2, one)
                stats = one if h == 0 else stats + pltpu.roll(one, 64, 1)
            psend[j, g, :, 256:] = stats.astype(BF16)
            here = jnp.logical_and(j == s, grp == g)

            @pl.when(jnp.logical_not(here))
            def _():
                send(psend.at[j, g], pbuf.at[mine], p_send.at[j * 2 + g], p_recv.at[mine], at(g, z * 4 + j))

            @pl.when(here)
            def _():
                pbuf[mine] = psend[j, g]

        return carry

    lax.fori_loop(1, 5, last, 0)

    for n in range(4):
        source = (n // 2) * 8 + 2 * z + n % 2

        @pl.when(source != tp)
        def _():
            arrive(fresh_in.at[n], x_send.at[0], f_recv.at[n])

    own_key = fresh_in[0].astype(F32) + fresh_in[1].astype(F32)
    own_value = fresh_in[2].astype(F32) + fresh_in[3].astype(F32)
    for n in range(1, 8):
        index = (mine + n) % 8
        arrive(pbuf.at[index], x_send.at[0], p_recv.at[index])
    half = slots_ref.shape[1]
    document = column(doc_ref)
    holder = jnp.where(document == 0, slots_ref[0, 0] // half, slots_ref[1, 0] // half)
    holder = jnp.concatenate([holder] * 3, axis=1)
    narrow = lanes((rows, 128))
    value_up = ku_ref[:, :, pl.ds(pl.multiple_of(512 + z * 128, 128), 128)].reshape(256, 128)
    row_of = lax.broadcasted_iota(jnp.int32, (128, 256), 0)
    tile = (row_of == lanes((128, 256)) % 16).astype(F32).astype(BF16)
    blocks = [
        jnp.where(holder == 0, pbuf[j].astype(F32), pbuf[4 + j].astype(F32)) for j in range(4)
    ]
    for h in range(2):
        query = qbuf[mine, :, h * 128 : (h + 1) * 128].astype(F32)
        own = jnp.sum(query * own_key, axis=-1, keepdims=True) * scale
        top = own
        parts = []
        for block in blocks:
            stats = block[:, 256:]
            if h:
                stats = pltpu.roll(stats, 64, 1)
            at_peak = jnp.logical_and(narrow >= 24, narrow < 27)
            m = jnp.sum(jnp.where(at_peak, stats, 0.0), axis=-1, keepdims=True)
            tail = jnp.where(narrow < 17, stats + pltpu.roll(stats, 96, 1), 0.0)
            top = jnp.maximum(top, m)
            parts.append((block[:, h * 128 : (h + 1) * 128], tail, m))
        own_weight = jnp.exp2(own - top)
        numerator = own_weight * own_value
        tail_sum = jnp.zeros((rows, 128), F32)
        for num, tail, m in parts:
            weight = jnp.exp2(m - top)
            numerator = numerator + num * weight
            tail_sum = tail_sum + tail * weight
        total = jnp.sum(jnp.where(narrow == 16, tail_sum, 0.0), axis=-1, keepdims=True) + own_weight
        factor = jnp.where(narrow < 16, tail_sum, 0.0)
        high = factor.astype(BF16)
        shift = jnp.zeros((rows, 128), F32)
        for piece in (high, (factor - high.astype(F32)).astype(BF16)):
            expanded = jnp.where(picked, dot(piece, tile), 0.0).astype(BF16)
            shift = shift + dot(expanded, value_up)
        out_ref[:, h * 128 : (h + 1) * 128] = ((numerator + shift) / total).astype(BF16)

    for copy in started:
        copy.wait_send()
    for j in range(4):
        target = head * 4 + j

        @pl.when(target != tp)
        def _():
            pltpu.make_async_remote_copy(
                src_ref=fresh, dst_ref=fresh_in.at[slot], send_sem=f_send.at[j],
                recv_sem=f_recv.at[slot], device_id=at(grp, target), device_id_type=MESH,
            ).wait_send()

    for j in range(4):
        for g in range(2):

            @pl.when(jnp.logical_not(jnp.logical_and(j == s, grp == g)))
            def _():
                pltpu.make_async_remote_copy(
                    src_ref=psend.at[j, g], dst_ref=pbuf.at[mine], send_sem=p_send.at[j * 2 + g],
                    recv_sem=p_recv.at[mine], device_id=at(g, z * 4 + j), device_id_type=MESH,
                ).wait_send()


def fused_device(
    residual_input, input_norm_gain, query_weight, key_value_weight, shared_down_factors,
    query_up_factors, key_value_up_factors, paged_base_keys, paged_base_values,
    paged_down_factors, adapter_of_row, document_of_row, document_page_slots,
):
    rows, chunk = residual_input.shape
    vmem = pl.BlockSpec(memory_space=pltpu.VMEM)
    hbm = pl.BlockSpec(memory_space=pltpu.HBM)
    smem = pl.BlockSpec(memory_space=pltpu.SMEM)
    dma = pltpu.SemaphoreType.DMA
    width = 16 * chunk
    return pl.pallas_call(
        fused_kernel,
        out_shape=jax.ShapeDtypeStruct((rows, 256), BF16),
        in_specs=[vmem, vmem, hbm, hbm, hbm, hbm, hbm, hbm, hbm, vmem, vmem, vmem, smem],
        out_specs=vmem,
        scratch_shapes=[
            pltpu.VMEM((16, rows, 384), BF16),
            pltpu.VMEM((width, 256), BF16),
            pltpu.VMEM((64, width), BF16),
            pltpu.VMEM((48, width), BF16),
            pltpu.VMEM((16, 16, 256), BF16),
            pltpu.VMEM((16, 16, 1024), BF16),
            pltpu.VMEM((width, 128), BF16),
            pltpu.VMEM((rows, 256), F32),
            pltpu.VMEM((rows, 128), F32),
            pltpu.VMEM((rows, 1), F32),
            pltpu.VMEM((4, 4, 128, 128), BF16),
            pltpu.VMEM((4, 4, 128, 128), BF16),
            pltpu.VMEM((4, 128, 128), BF16),
            pltpu.VMEM((8, rows, 384), BF16),
            pltpu.VMEM((4, 4 * rows, 256), BF16),
            pltpu.VMEM((512, 256), BF16),
            pltpu.VMEM((512, 256), BF16),
            pltpu.VMEM((4, 4 * rows, 256), F32),
            pltpu.VMEM((4, 4 * rows, 1), F32),
            pltpu.VMEM((4, 2, rows, 384), BF16),
            pltpu.VMEM((8, rows, 384), BF16),
            pltpu.VMEM((rows, 128), BF16),
            pltpu.VMEM((4, rows, 128), BF16),
            dma((7,)), dma((16,)), dma((16,)), dma((9,)), dma((12,)),
            dma((7,)), dma((8,)), dma((4,)), dma((4,)), dma((8,)), dma((8,)),
        ],
        compiler_params=pltpu.CompilerParams(
            collective_id=0, has_side_effects=True, vmem_limit_bytes=63 * 1024 * 1024
        ),
        cost_estimate=pl.CostEstimate(
            flops=5_000_000_000, bytes_accessed=8_000_000, transcendentals=4_500_000
        ),
    )(
        residual_input.T, input_norm_gain.reshape(1, width), query_weight, key_value_weight.T,
        shared_down_factors.T, query_up_factors, key_value_up_factors, paged_base_keys,
        paged_base_values, paged_down_factors.transpose(0, 2, 1), adapter_of_row.reshape(1, rows),
        document_of_row.reshape(1, rows), document_page_slots,
    )


def merge_slices(numerator, factor_sum, maxima, totals):
    peak_all = jnp.max(maxima, axis=-1)
    weight = jnp.exp(maxima - peak_all[..., None])
    numerator = jnp.sum(numerator * weight[..., None], axis=-2)
    factor_sum = jnp.sum(factor_sum * weight[..., None], axis=-2)
    totals = jnp.sum(totals * weight, axis=-1)
    return (numerator, factor_sum, peak_all, totals)


def attend_local(
    query_matrix,
    down_factors,
    paged_base_keys,
    paged_base_values,
    paged_down_factors,
    heads_kv,
    low_rank_width,
):
    item_count = query_matrix.shape[0]
    head_size = paged_base_keys.shape[-1] // heads_kv
    all_heads = query_matrix.shape[1] // head_size
    query_group_size = all_heads // heads_kv
    local_tokens = paged_base_keys.shape[0] * paged_base_keys.shape[1]
    score_scaling = head_size ** (-0.5)
    key_heads = paged_base_keys.reshape(local_tokens, heads_kv, head_size).transpose(1, 0, 2)
    value_heads = paged_base_values.reshape(local_tokens, heads_kv, head_size).transpose(1, 0, 2)
    factor_flat = paged_down_factors.reshape(local_tokens, 2 * low_rank_width)
    cached_key = factor_flat[:, :low_rank_width]
    cached_value = factor_flat[:, low_rank_width:]
    query_head_count = query_matrix.reshape(
        item_count, heads_kv, query_group_size, head_size
    ).transpose(1, 0, 2, 3)
    factor_heads = down_factors.reshape(
        item_count, heads_kv, query_group_size, low_rank_width
    ).transpose(1, 0, 2, 3)

    def one_head(bundle):
        query_one, factor_one, key_one, value_one = bundle
        scores = (
            jnp.einsum("ngd,ld->ngl", query_one, key_one, preferred_element_type=jnp.float32)
            + jnp.einsum("ngj,lj->ngl", factor_one, cached_key, preferred_element_type=jnp.float32)
        ) * score_scaling
        maxima = jnp.max(scores, -1)
        weights = jnp.exp(scores - maxima[..., None])
        totals = jnp.sum(weights, -1)
        rounded = weights.astype(jnp.bfloat16)
        numerator = jnp.einsum(
            "ngl,ld->ngd", rounded, value_one, preferred_element_type=jnp.float32
        )
        factor_sum = jnp.einsum(
            "ngl,lj->ngj", rounded, cached_value, preferred_element_type=jnp.float32
        )
        return (numerator, factor_sum, maxima, totals)

    numerator, factor_sum, maxima, totals = lax.map(
        one_head, (query_head_count, factor_heads, key_heads, value_heads)
    )
    numerator = numerator.transpose(1, 0, 2, 3).reshape(item_count, all_heads, head_size)
    factor_sum = factor_sum.transpose(1, 0, 2, 3).reshape(item_count, all_heads, low_rank_width)
    maxima = maxima.transpose(1, 0, 2).reshape(item_count, all_heads)
    totals = totals.transpose(1, 0, 2).reshape(item_count, all_heads)
    return (numerator, factor_sum, maxima, totals)


def per_device(
    residual_input,
    input_norm_gain,
    query_weight,
    key_value_weight,
    shared_down_factors,
    query_up_factors,
    key_value_up_factors,
    paged_base_keys,
    paged_base_values,
    paged_down_factors,
    adapter_of_row,
    document_of_row,
    document_page_slots,
):
    tp_count = lax.axis_size("tp")
    grp_count = lax.axis_size("grp")
    tp_index = lax.axis_index("tp")
    low_rank_width = shared_down_factors.shape[1] // 3
    key_value_width = key_value_up_factors.shape[2] // 2
    head_size = HEAD_SIZE
    heads_kv = key_value_width // head_size
    row_count = residual_input.shape[0]
    score_scaling = head_size ** (-0.5)
    gathered = lax.all_gather(residual_input, "tp", axis=1, tiled=True).astype(jnp.float32)
    normed_input = (
        gathered
        * lax.rsqrt(jnp.mean(gathered * gathered, -1, keepdims=True) + 1e-06)
        * input_norm_gain
    ).astype(jnp.bfloat16)
    low_rank_part = jnp.dot(
        normed_input, shared_down_factors, preferred_element_type=jnp.float32
    ).astype(jnp.bfloat16)
    query_low_rank = low_rank_part[:, :low_rank_width]
    key_low_rank = low_rank_part[:, low_rank_width : 2 * low_rank_width]
    value_low_rank = low_rank_part[:, 2 * low_rank_width :]
    query_update = query_up_factors[adapter_of_row]
    query_part = (
        jnp.dot(normed_input, query_weight, preferred_element_type=jnp.float32)
        + jnp.einsum("ep,epg->eg", query_low_rank, query_update, preferred_element_type=jnp.float32)
    ).astype(jnp.bfloat16)
    key_value_columns = key_value_weight.shape[1]
    key_value_start = tp_index * key_value_columns
    key_value_update = lax.dynamic_slice_in_dim(
        key_value_up_factors, key_value_start, key_value_columns, 2
    )[adapter_of_row]
    key_value_low = jnp.where(key_value_start < key_value_width, key_low_rank, value_low_rank)
    kv_part = (
        jnp.dot(normed_input, key_value_weight, preferred_element_type=jnp.float32)
        + jnp.einsum(
            "ep,epg->eg", key_value_low, key_value_update, preferred_element_type=jnp.float32
        )
    ).astype(jnp.bfloat16)
    heads_here = query_part.shape[1] // head_size
    query_group_size = heads_here * tp_count // heads_kv
    key_value_head = tp_index * heads_here // query_group_size
    key_column_count = lax.dynamic_slice_in_dim(
        key_value_up_factors, key_value_head * head_size, head_size, 2
    )[adapter_of_row]
    my_queries = query_part.reshape(row_count, heads_here, head_size)
    factor_part = jnp.einsum(
        "rhd,rjd->rhj", my_queries, key_column_count, preferred_element_type=jnp.float32
    ).astype(jnp.bfloat16)
    factor_part = factor_part.reshape(row_count, heads_here * low_rank_width)
    query_matrix, down_factors, fresh_kv = (
        lax.all_gather(query_part, "tp", axis=1, tiled=True),
        lax.all_gather(factor_part, "tp", axis=1, tiled=True),
        lax.all_gather(kv_part, "tp", axis=1, tiled=True),
    )
    doc_pages = document_page_slots.shape[1]
    owner_of_doc = document_page_slots[:, 0] // doc_pages
    doc_ids = document_of_row[:, 0]
    doc_match = (doc_ids[:, None] == jnp.arange(document_page_slots.shape[0])[None, :]).astype(
        jnp.int32
    )
    target = jnp.sum(doc_match * owner_of_doc[None, :], 1)
    target_match = (target[:, None] == jnp.arange(grp_count)[None, :]).astype(jnp.int32)
    earlier = jnp.cumsum(target_match, 0) - target_match
    capacity = 2 * row_count // grp_count
    slot_of = target * capacity + jnp.sum(earlier * target_match, 1)
    placing = (jnp.arange(grp_count * capacity)[:, None] == slot_of[None, :]).astype(jnp.bfloat16)
    send_queries = (
        jnp.dot(placing, query_matrix, preferred_element_type=jnp.float32)
        .astype(jnp.bfloat16)
        .reshape(grp_count, capacity, -1)
    )
    send_factors = (
        jnp.dot(placing, down_factors, preferred_element_type=jnp.float32)
        .astype(jnp.bfloat16)
        .reshape(grp_count, capacity, -1)
    )
    query_in = lax.all_to_all(send_queries, "grp", split_axis=0, concat_axis=0, tiled=True)
    factor_in = lax.all_to_all(send_factors, "grp", split_axis=0, concat_axis=0, tiled=True)
    per_source = query_in.shape[1]
    item_count = query_in.shape[0] * per_source
    query_flat = query_in.reshape(item_count, -1)
    factor_flat = factor_in.reshape(item_count, -1)
    numerator, factor_sum, maxima, totals = attend_local(
        query_flat,
        factor_flat,
        paged_base_keys,
        paged_base_values,
        paged_down_factors,
        heads_kv,
        low_rank_width,
    )
    all_heads = numerator.shape[1]
    returned = (
        lax.all_to_all(
            numerator.reshape(grp_count, per_source, all_heads, head_size),
            "grp",
            split_axis=0,
            concat_axis=0,
            tiled=True,
        ),
        lax.all_to_all(
            factor_sum.reshape(grp_count, per_source, all_heads, low_rank_width),
            "grp",
            split_axis=0,
            concat_axis=0,
            tiled=True,
        ),
        lax.all_to_all(
            maxima.reshape(grp_count, per_source, all_heads),
            "grp",
            split_axis=0,
            concat_axis=0,
            tiled=True,
        ),
        lax.all_to_all(
            totals.reshape(grp_count, per_source, all_heads),
            "grp",
            split_axis=0,
            concat_axis=0,
            tiled=True,
        ),
    )
    numerator, factor_sum, maxima, totals = [
        piece.reshape((grp_count * capacity,) + piece.shape[2:])[slot_of] for piece in returned
    ]
    numerator, factor_sum, maxima, totals = (
        lax.all_to_all(numerator[:, :, None, :], "tp", split_axis=1, concat_axis=2, tiled=True),
        lax.all_to_all(factor_sum[:, :, None, :], "tp", split_axis=1, concat_axis=2, tiled=True),
        lax.all_to_all(maxima[:, :, None], "tp", split_axis=1, concat_axis=2, tiled=True),
        lax.all_to_all(totals[:, :, None], "tp", split_axis=1, concat_axis=2, tiled=True),
    )
    numerator, factor_sum, maxima, totals = merge_slices(numerator, factor_sum, maxima, totals)
    own_key = lax.dynamic_slice_in_dim(fresh_kv, key_value_head * head_size, head_size, 1)
    value_own = lax.dynamic_slice_in_dim(
        fresh_kv, key_value_width + key_value_head * head_size, head_size, 1
    )
    own_token_score = (
        jnp.einsum("rhd,rd->rh", my_queries, own_key, preferred_element_type=jnp.float32)
        * score_scaling
    )
    peak_all = jnp.maximum(maxima, own_token_score)
    old_scale = jnp.exp(maxima - peak_all)
    own_weight = jnp.exp(own_token_score - peak_all)
    numerator = (
        numerator * old_scale[..., None]
        + own_weight[..., None] * value_own.astype(jnp.float32)[:, None, :]
    )
    factor_sum = factor_sum * old_scale[..., None]
    totals = totals * old_scale + own_weight
    value_column_count = lax.dynamic_slice_in_dim(
        key_value_up_factors, key_value_width + key_value_head * head_size, head_size, 2
    )[adapter_of_row]
    value_shift = jnp.einsum(
        "rhj,rjd->rhd",
        factor_sum,
        value_column_count.astype(jnp.float32),
        precision=lax.Precision.HIGHEST,
    )
    result = ((numerator + value_shift) / totals[..., None]).astype(jnp.bfloat16)
    return result.reshape(row_count, heads_here * head_size)


def solution(mesh):
    in_specs = (
        P("grp", "tp"),
        P(),
        P(None, "tp"),
        P(None, "tp"),
        P(),
        P(None, None, "tp"),
        P(),
        P(("grp", "tp"), None, None),
        P(("grp", "tp"), None, None),
        P(("grp", "tp"), None, None),
        P("grp"),
        P("grp", None),
        P(),
    )
    out_specs = P("grp", "tp")
    fits = mesh.shape["grp"] == 2 and mesh.shape["tp"] == 16
    return jax.shard_map(
        fused_device if fits else per_device, mesh=mesh, in_specs=in_specs, out_specs=out_specs, check_vma=False
    )
```

```python
import functools
import math

import jax
import jax.numpy as jnp
from jax import lax
from jax.experimental import pallas as pl
from jax.experimental.pallas import tpu as pltpu
from jax.sharding import PartitionSpec as P

HEAD_SIZE = 128
MESH = pl.DeviceIdType.MESH
F32 = jnp.float32
BF16 = jnp.bfloat16


def dot(a, b):
    return jnp.dot(a, b, preferred_element_type=F32)


def dot_nt(a, b):
    return lax.dot_general(a, b, (((1,), (1,)), ((), ())), preferred_element_type=F32)


def lanes(shape):
    return lax.broadcasted_iota(jnp.int32, shape, len(shape) - 1)


def split_three(value):
    high = value.astype(BF16).astype(F32)
    middle = (value - high).astype(BF16).astype(F32)
    low = (value - high - middle).astype(BF16).astype(F32)
    return high, middle, low


def fused_kernel(
    x_ref, gain_ref, qw_hbm, kvw_hbm, dn_hbm, qu_hbm, ku_hbm, k_hbm, v_hbm, d_ref,
    adapter_ref, doc_ref, slots_ref, out_ref,
    xbuf, qw, kvw, dn, qu_ref, ku_ref, wo, yq, yo, ssq, kbuf, vbuf, dbuf, qbuf, qcol, kaug, vaug, vup,
    acc, peak, psend, pbuf, fresh, fresh_in,
    load_sem, x_send, x_recv, kv_send, kv_recv, q_send, q_recv, f_send, f_recv, p_send, p_recv,
):
    chunk, rows = x_ref.shape
    width = 16 * chunk
    grp = lax.axis_index("grp")
    tp = lax.axis_index("tp")
    z = tp // 4
    s = tp % 4
    y = s // 2
    c = s % 2
    scale = math.log2(math.e) / math.sqrt(HEAD_SIZE)

    def at(g, t):
        return {"grp": g, "tp": t}

    sibling = at(grp, z * 4 + y * 2 + (1 - c))
    across = at(grp, z * 4 + (1 - y) * 2 + c)
    z_others = [z + 1 - 2 * (z % 2), (z + 2) % 4, 3 - z]

    loads = [
        pltpu.make_async_copy(src, dst, load_sem.at[i])
        for i, (src, dst) in enumerate(
            ((kvw_hbm, kvw), (dn_hbm, dn), (qw_hbm, qw),
             (k_hbm.at[:, :, pl.ds(pl.multiple_of(z * 128, 128), 128)], kbuf.at[z]),
             (v_hbm.at[:, :, pl.ds(pl.multiple_of(z * 128, 128), 128)], vbuf.at[z]),
             (qu_hbm, qu_ref), (ku_hbm, ku_ref))
        )
    ]
    for load in loads:
        load.start()

    barrier = pltpu.get_barrier_semaphore()
    for i in range(1, 16):
        pl.semaphore_signal(barrier, inc=1, device_id=at(grp, (tp + i) % 16), device_id_type=MESH)
    for j in range(4):
        pl.semaphore_signal(barrier, inc=1, device_id=at(1 - grp, z * 4 + j), device_id_type=MESH)
    dbuf[z] = d_ref[...].reshape(128, 128)
    gain = jnp.zeros((1, chunk), F32)
    for t in range(16):
        gain = gain + jnp.where(tp == t, gain_ref[:, t * chunk : (t + 1) * chunk], 0.0)
    x_rows = x_ref[...].T.astype(F32)
    pieces = split_three(jnp.sum(x_rows * x_rows, axis=-1, keepdims=True))
    xbuf[tp, :, :chunk] = (x_rows * gain).astype(BF16)
    spare = lanes((rows, 384 - chunk))
    sums = jnp.zeros(spare.shape, F32)
    for i, piece in enumerate(pieces):
        sums = jnp.where(spare == i, piece, sums)
    xbuf[tp, :, chunk:] = sums.astype(BF16)
    pl.semaphore_wait(barrier, 19)

    started = []

    def send(src, dst, send_sem, recv_sem, device):
        copy = pltpu.make_async_remote_copy(
            src_ref=src, dst_ref=dst, send_sem=send_sem, recv_sem=recv_sem,
            device_id=device, device_id_type=MESH,
        )
        copy.start()
        return copy

    def arrive(dst, send_sem, recv_sem):
        pltpu.make_async_remote_copy(
            src_ref=dst, dst_ref=dst, send_sem=send_sem, recv_sem=recv_sem,
            device_id=sibling, device_id_type=MESH,
        ).wait_recv()

    def send_x(t, sem, device):
        copy = send(xbuf.at[t], xbuf.at[t], x_send.at[sem], x_recv.at[t], device)
        started.append(copy)
        return copy

    def send_q(index, sem, device):
        started.append(send(qbuf.at[index], qbuf.at[index], q_send.at[sem], q_recv.at[index], device))

    send_x(tp, 0, at(grp, z_others[1] * 4 + s))
    send_x(tp, 1, at(grp, z_others[0] * 4 + s))
    send_x(tp, 3, across)
    send_x(tp, 7, sibling)
    for i in (1, 2, 0):
        zo = z_others[i]
        cols = pl.ds(pl.multiple_of(zo * 128, 128), 128)
        device = at(grp, zo * 4 + s)
        for n2, (src, dst) in enumerate(
            ((k_hbm.at[:, :, cols], kbuf), (v_hbm.at[:, :, cols], vbuf), (dbuf.at[z], dbuf))
        ):
            started.append(
                send(src, dst.at[z], kv_send.at[i * 3 + n2], kv_recv.at[z * 3 + n2], device)
            )

    loads[0].wait()
    loads[1].wait()

    def join(i, carry):
        part = pl.ds(pl.multiple_of(i * 128, 128), 128)
        both = jnp.concatenate([kvw[:, part], dn[:, part], jnp.zeros((16, 128), BF16)], axis=0)
        wo[part, :] = both.T
        return carry

    lax.fori_loop(0, width // 128, join, 0)
    yq[...] = jnp.zeros_like(yq)
    yo[...] = jnp.zeros_like(yo)
    ssq[...] = jnp.zeros_like(ssq)
    loads[2].wait()

    def project(t):
        scaled = xbuf[t, :, :chunk]
        ssq[...] += jnp.sum(xbuf[t, :, chunk:].astype(F32), axis=-1, keepdims=True)
        part = pl.ds(pl.multiple_of(t * chunk, 64), chunk)
        yq[...] += dot(scaled, qw[part, :])
        yo[...] += dot(scaled, wo[part, :])

    def augment(zo):
        down = dbuf[zo].astype(F32).T.astype(BF16)
        for p in range(4):
            part = pl.ds(p * 128, 128)
            kaug[zo, part, :128] = kbuf[zo, p]
            kaug[zo, part, 128:] = jnp.concatenate(
                [down[:, p * 32 : p * 32 + 16], jnp.zeros((128, 112), BF16)], axis=1
            )
            vaug[zo, :128, part] = vbuf[zo, p].T
            vaug[zo, 128:144, part] = dbuf[zo, p * 32 + 16 : p * 32 + 32, :]
        first_row = lax.broadcasted_iota(jnp.int32, (16, 512), 0) == 0
        vaug[zo, 144:, :] = first_row.astype(F32).astype(BF16)

    def attend(zo, j, start):
        scores = dot(kaug[zo], qcol[j])
        top = jnp.max(scores, axis=0, keepdims=True) * scale
        if not start:
            old = peak[j]
            top = jnp.maximum(old, top)
        weights = jnp.exp2(scores * scale - top).astype(BF16)
        product = dot(vaug[zo], weights)
        if start:
            acc[j] = product
        else:
            acc[j] = acc[j] * jnp.exp2(old - top) + product
        peak[j] = top

    project(tp)
    loads[3].wait()
    loads[4].wait()
    loads[5].wait()
    loads[6].wait()
    augment(z)
    qcol[:, 144:, :] = jnp.zeros((4, 112, 512), BF16)
    vup[...] = (
        ku_ref[:, :, pl.ds(pl.multiple_of(512 + z * 128, 128), 128)].reshape(256, 128).T
    )
    for i in (1, 0, 2):
        t = z_others[i] * 4 + s
        arrive(xbuf.at[t], x_send.at[0], x_recv.at[t])
        if i == 1:
            send_x(t, 2, at(grp, z_others[0] * 4 + s))
        send_x(t, 4 + i, across)
        send_x(t, 8 + i, sibling)
        project(t)
    for i, zo in enumerate([z] + z_others):
        t = zo * 4 + (1 - y) * 2 + c
        arrive(xbuf.at[t], x_send.at[0], x_recv.at[t])
        send_x(t, 11 + i, sibling)
        project(t)
    for zo in [z] + z_others:
        for yo_ in (y, 1 - y):
            t = zo * 4 + yo_ * 2 + (1 - c)
            arrive(xbuf.at[t], x_send.at[0], x_recv.at[t])
            project(t)

    rinv = lax.rsqrt(ssq[...] * (1.0 / width) + 1e-06)
    other = yo[...] * rinv
    low = other[:, 64:128].astype(BF16)
    def column(row_ref):
        return jnp.broadcast_to(row_ref[...].astype(F32), (rows, rows)).T.astype(jnp.int32)

    adapter = column(adapter_ref)
    adapter = jnp.concatenate([adapter, adapter], axis=1)
    wide = lanes((rows, 256))
    picked = (wide // 16) == adapter
    row_of = lax.broadcasted_iota(jnp.int32, (64, 256), 0)
    col_of = lanes((64, 256)) % 16

    def spread(part, offset):
        tile = (row_of == col_of + offset).astype(F32).astype(BF16)
        return jnp.where(picked, dot(part, tile), 0.0).astype(BF16)

    queries = (yq[...] * rinv + dot(spread(low, 0), qu_ref[...].reshape(256, 256))).astype(BF16)
    odd = tp % 2
    is_key = tp < 8
    kv_low = jnp.where(is_key, spread(low, 16).astype(F32), spread(low, 32).astype(F32)).astype(BF16)
    pair_cols = pl.ds(pl.multiple_of((tp // 2) * 128, 128), 128)
    kv_update = dot(kv_low, ku_ref[:, :, pair_cols].reshape(256, 128))
    kv_base = other[:, :64]
    kv_full = (jnp.concatenate([kv_base, kv_base], axis=1) + kv_update).T
    fresh[...] = jnp.where(odd == 1, kv_full[64:], kv_full[:64]).astype(BF16)
    fold_row = lax.broadcasted_iota(jnp.int32, (256, 128), 0) % 16
    fold_col = lanes((256, 128))
    key_up = ku_ref[:, :, pl.ds(pl.multiple_of(z * 128, 128), 128)].reshape(256, 128)
    factors = jnp.zeros((rows, 128), F32)
    for h in range(2):
        full = dot_nt(queries[:, h * 128 : (h + 1) * 128], key_up)
        full = jnp.where(picked, full, 0.0).astype(BF16)
        fold = (fold_col == fold_row + 16 * h).astype(F32).astype(BF16)
        factors = factors + dot(full, fold)
    mine = 4 * grp + s
    qbuf[mine, :256, :] = queries.astype(F32).T.astype(BF16)
    qbuf[mine, 256:, :] = factors.T[:32].astype(BF16)

    far = (1 - y) * 2 + c
    direct = [(grp, far), (1 - grp, s), (1 - grp, far)]
    for n, (g, j) in enumerate(direct):
        send_q(mine, n, at(g, z * 4 + j))
    send_q(mine, 3, sibling)
    head = (tp % 8) // 2
    slot = (tp // 8) * 2 + odd
    for j in range(4):
        target = head * 4 + j

        @pl.when(target != tp)
        def _():
            send(fresh, fresh_in.at[slot], f_send.at[j], f_recv.at[slot], at(grp, target))

        @pl.when(target == tp)
        def _():
            fresh_in[slot] = fresh[...]

    for n, (g, j) in enumerate(direct):
        index = 4 * g + j
        arrive(qbuf.at[index], x_send.at[0], q_recv.at[index])
        send_q(index, 4 + n, sibling)
    for j, waited in ((s, True), (far, True), (y * 2 + 1 - c, False), (3 - s, False)):
        for g in (grp, 1 - grp):
            index = 4 * g + j
            if not waited:
                arrive(qbuf.at[index], x_send.at[0], q_recv.at[index])
            for h in range(2):
                part = pl.ds(pl.multiple_of(h * 256 + g * 128, 128), 128)
                qcol[j, :128, part] = qbuf[index, h * 128 : (h + 1) * 128, :]
                qcol[j, 128:144, part] = qbuf[index, 256 + h * 16 : 272 + h * 16, :]
        attend(z, j, True)

    def arrived(zo):
        for n2, dst in enumerate((kbuf, vbuf, dbuf)):
            arrive(dst.at[zo], x_send.at[0], kv_recv.at[zo * 3 + n2])

    for zo in z_others[:2]:
        arrived(zo)
        augment(zo)

        def body(j, carry):
            attend(zo, j, False)
            return carry

        lax.fori_loop(0, 4, body, 0)

    arrived(z_others[2])
    augment(z_others[2])

    def last(shift, carry):
        j = (s + shift) % 4
        attend(z_others[2], j, False)
        line = lax.broadcasted_iota(jnp.int32, (16, 128), 0)
        for g in range(2):
            for h in range(2):
                part = pl.ds(h * 256 + g * 128, 128)
                psend[j, g, h * 128 : (h + 1) * 128, :] = acc[j, :128, part].astype(BF16)
                psend[j, g, 256 + h * 32 : 272 + h * 32, :] = acc[j, 128:144, part].astype(BF16)
                stats = jnp.zeros((16, 128), F32)
                pieces = split_three(acc[j, 144:145, part])[:2] + split_three(peak[j, :, part])
                for i, piece in enumerate(pieces):
                    stats = jnp.where(line == i, piece, stats)
                psend[j, g, 272 + h * 32 : 288 + h * 32, :] = stats.astype(BF16)
            here = jnp.logical_and(j == s, grp == g)

            @pl.when(jnp.logical_not(here))
            def _():
                send(psend.at[j, g], pbuf.at[mine], p_send.at[j * 2 + g], p_recv.at[mine], at(g, z * 4 + j))

            @pl.when(here)
            def _():
                pbuf[mine] = psend[j, g]

        return carry

    lax.fori_loop(1, 5, last, 0)

    for n in range(4):
        source = (n // 2) * 8 + 2 * z + n % 2

        @pl.when(source != tp)
        def _():
            arrive(fresh_in.at[n], x_send.at[0], f_recv.at[n])

    own_key = jnp.concatenate([fresh_in[0], fresh_in[1]], axis=0).astype(F32)
    own_value = jnp.concatenate([fresh_in[2], fresh_in[3]], axis=0).astype(F32)
    for n in range(1, 8):
        index = (mine + n) % 8
        arrive(pbuf.at[index], x_send.at[0], p_recv.at[index])
    half = slots_ref.shape[1]
    holder = jnp.where(doc_ref[...] == 0, slots_ref[0, 0] // half, slots_ref[1, 0] // half)
    picked = lax.broadcasted_iota(jnp.int32, (256, rows), 0) // 16 == adapter_ref[...]
    blocks = [
        jnp.where(holder == 0, pbuf[j].astype(F32), pbuf[4 + j].astype(F32)) for j in range(4)
    ]
    for h in range(2):
        query = qbuf[mine, h * 128 : (h + 1) * 128, :].astype(F32)
        own = jnp.sum(query * own_key, axis=0, keepdims=True) * scale
        base = 256 + h * 32
        peaks = [b[base + 18 : base + 19] + b[base + 19 : base + 20] + b[base + 20 : base + 21] for b in blocks]
        top = own
        for m in peaks:
            top = jnp.maximum(top, m)
        total = jnp.exp2(own - top)
        numerator = total * own_value
        factor = jnp.zeros((16, rows), F32)
        for block, m in zip(blocks, peaks):
            weight = jnp.exp2(m - top)
            numerator = numerator + block[h * 128 : (h + 1) * 128] * weight
            factor = factor + block[base : base + 16] * weight
            total = total + (block[base + 16 : base + 17] + block[base + 17 : base + 18]) * weight
        expanded = jnp.where(picked, jnp.concatenate([factor] * 16, axis=0), 0.0)
        high = expanded.astype(BF16)
        shift = dot(vup[...], high) + dot(vup[...], (expanded - high.astype(F32)).astype(BF16))
        out_ref[:, h * 128 : (h + 1) * 128] = ((numerator + shift) / total).T.astype(BF16)

    for copy in started:
        copy.wait_send()
    for j in range(4):
        target = head * 4 + j

        @pl.when(target != tp)
        def _():
            pltpu.make_async_remote_copy(
                src_ref=fresh, dst_ref=fresh_in.at[slot], send_sem=f_send.at[j],
                recv_sem=f_recv.at[slot], device_id=at(grp, target), device_id_type=MESH,
            ).wait_send()

    for j in range(4):
        for g in range(2):

            @pl.when(jnp.logical_not(jnp.logical_and(j == s, grp == g)))
            def _():
                pltpu.make_async_remote_copy(
                    src_ref=psend.at[j, g], dst_ref=pbuf.at[mine], send_sem=p_send.at[j * 2 + g],
                    recv_sem=p_recv.at[mine], device_id=at(g, z * 4 + j), device_id_type=MESH,
                ).wait_send()


def fused_device(
    residual_input, input_norm_gain, query_weight, key_value_weight, shared_down_factors,
    query_up_factors, key_value_up_factors, paged_base_keys, paged_base_values,
    paged_down_factors, adapter_of_row, document_of_row, document_page_slots,
):
    rows, chunk = residual_input.shape
    vmem = pl.BlockSpec(memory_space=pltpu.VMEM)
    hbm = pl.BlockSpec(memory_space=pltpu.HBM)
    smem = pl.BlockSpec(memory_space=pltpu.SMEM)
    dma = pltpu.SemaphoreType.DMA
    width = 16 * chunk
    return pl.pallas_call(
        fused_kernel,
        out_shape=jax.ShapeDtypeStruct((rows, 256), BF16),
        in_specs=[vmem, vmem, hbm, hbm, hbm, hbm, hbm, hbm, hbm, vmem, vmem, vmem, smem],
        out_specs=vmem,
        scratch_shapes=[
            pltpu.VMEM((16, rows, 384), BF16),
            pltpu.VMEM((width, 256), BF16),
            pltpu.VMEM((64, width), BF16),
            pltpu.VMEM((48, width), BF16),
            pltpu.VMEM((16, 16, 256), BF16),
            pltpu.VMEM((16, 16, 1024), BF16),
            pltpu.VMEM((width, 128), BF16),
            pltpu.VMEM((rows, 256), F32),
            pltpu.VMEM((rows, 128), F32),
            pltpu.VMEM((rows, 1), F32),
            pltpu.VMEM((4, 4, 128, 128), BF16),
            pltpu.VMEM((4, 4, 128, 128), BF16),
            pltpu.VMEM((4, 128, 128), BF16),
            pltpu.VMEM((8, 288, rows), BF16),
            pltpu.VMEM((4, 256, 4 * rows), BF16),
            pltpu.VMEM((4, 512, 256), BF16),
            pltpu.VMEM((4, 160, 512), BF16),
            pltpu.VMEM((128, 256), BF16),
            pltpu.VMEM((4, 160, 4 * rows), F32),
            pltpu.VMEM((4, 1, 4 * rows), F32),
            pltpu.VMEM((4, 2, 320, rows), BF16),
            pltpu.VMEM((8, 320, rows), BF16),
            pltpu.VMEM((64, rows), BF16),
            pltpu.VMEM((4, 64, rows), BF16),
            dma((7,)), dma((16,)), dma((16,)), dma((9,)), dma((12,)),
            dma((7,)), dma((8,)), dma((4,)), dma((4,)), dma((8,)), dma((8,)),
        ],
        compiler_params=pltpu.CompilerParams(
            collective_id=0, has_side_effects=True, vmem_limit_bytes=63 * 1024 * 1024
        ),
        cost_estimate=pl.CostEstimate(
            flops=5_000_000_000, bytes_accessed=8_000_000, transcendentals=4_500_000
        ),
    )(
        residual_input.T, input_norm_gain.reshape(1, width), query_weight, key_value_weight.T,
        shared_down_factors.T, query_up_factors, key_value_up_factors, paged_base_keys,
        paged_base_values, paged_down_factors.transpose(0, 2, 1), adapter_of_row.reshape(1, rows),
        document_of_row.reshape(1, rows), document_page_slots,
    )


def merge_slices(numerator, factor_sum, maxima, totals):
    peak_all = jnp.max(maxima, axis=-1)
    weight = jnp.exp(maxima - peak_all[..., None])
    numerator = jnp.sum(numerator * weight[..., None], axis=-2)
    factor_sum = jnp.sum(factor_sum * weight[..., None], axis=-2)
    totals = jnp.sum(totals * weight, axis=-1)
    return (numerator, factor_sum, peak_all, totals)


def attend_local(
    query_matrix,
    down_factors,
    paged_base_keys,
    paged_base_values,
    paged_down_factors,
    heads_kv,
    low_rank_width,
):
    item_count = query_matrix.shape[0]
    head_size = paged_base_keys.shape[-1] // heads_kv
    all_heads = query_matrix.shape[1] // head_size
    query_group_size = all_heads // heads_kv
    local_tokens = paged_base_keys.shape[0] * paged_base_keys.shape[1]
    score_scaling = head_size ** (-0.5)
    key_heads = paged_base_keys.reshape(local_tokens, heads_kv, head_size).transpose(1, 0, 2)
    value_heads = paged_base_values.reshape(local_tokens, heads_kv, head_size).transpose(1, 0, 2)
    factor_flat = paged_down_factors.reshape(local_tokens, 2 * low_rank_width)
    cached_key = factor_flat[:, :low_rank_width]
    cached_value = factor_flat[:, low_rank_width:]
    query_head_count = query_matrix.reshape(
        item_count, heads_kv, query_group_size, head_size
    ).transpose(1, 0, 2, 3)
    factor_heads = down_factors.reshape(
        item_count, heads_kv, query_group_size, low_rank_width
    ).transpose(1, 0, 2, 3)

    def one_head(bundle):
        query_one, factor_one, key_one, value_one = bundle
        scores = (
            jnp.einsum("ngd,ld->ngl", query_one, key_one, preferred_element_type=jnp.float32)
            + jnp.einsum("ngj,lj->ngl", factor_one, cached_key, preferred_element_type=jnp.float32)
        ) * score_scaling
        maxima = jnp.max(scores, -1)
        weights = jnp.exp(scores - maxima[..., None])
        totals = jnp.sum(weights, -1)
        rounded = weights.astype(jnp.bfloat16)
        numerator = jnp.einsum(
            "ngl,ld->ngd", rounded, value_one, preferred_element_type=jnp.float32
        )
        factor_sum = jnp.einsum(
            "ngl,lj->ngj", rounded, cached_value, preferred_element_type=jnp.float32
        )
        return (numerator, factor_sum, maxima, totals)

    numerator, factor_sum, maxima, totals = lax.map(
        one_head, (query_head_count, factor_heads, key_heads, value_heads)
    )
    numerator = numerator.transpose(1, 0, 2, 3).reshape(item_count, all_heads, head_size)
    factor_sum = factor_sum.transpose(1, 0, 2, 3).reshape(item_count, all_heads, low_rank_width)
    maxima = maxima.transpose(1, 0, 2).reshape(item_count, all_heads)
    totals = totals.transpose(1, 0, 2).reshape(item_count, all_heads)
    return (numerator, factor_sum, maxima, totals)


def per_device(
    residual_input,
    input_norm_gain,
    query_weight,
    key_value_weight,
    shared_down_factors,
    query_up_factors,
    key_value_up_factors,
    paged_base_keys,
    paged_base_values,
    paged_down_factors,
    adapter_of_row,
    document_of_row,
    document_page_slots,
):
    tp_count = lax.axis_size("tp")
    grp_count = lax.axis_size("grp")
    tp_index = lax.axis_index("tp")
    low_rank_width = shared_down_factors.shape[1] // 3
    key_value_width = key_value_up_factors.shape[2] // 2
    head_size = HEAD_SIZE
    heads_kv = key_value_width // head_size
    row_count = residual_input.shape[0]
    score_scaling = head_size ** (-0.5)
    gathered = lax.all_gather(residual_input, "tp", axis=1, tiled=True).astype(jnp.float32)
    normed_input = (
        gathered
        * lax.rsqrt(jnp.mean(gathered * gathered, -1, keepdims=True) + 1e-06)
        * input_norm_gain
    ).astype(jnp.bfloat16)
    low_rank_part = jnp.dot(
        normed_input, shared_down_factors, preferred_element_type=jnp.float32
    ).astype(jnp.bfloat16)
    query_low_rank = low_rank_part[:, :low_rank_width]
    key_low_rank = low_rank_part[:, low_rank_width : 2 * low_rank_width]
    value_low_rank = low_rank_part[:, 2 * low_rank_width :]
    query_update = query_up_factors[adapter_of_row]
    query_part = (
        jnp.dot(normed_input, query_weight, preferred_element_type=jnp.float32)
        + jnp.einsum("ep,epg->eg", query_low_rank, query_update, preferred_element_type=jnp.float32)
    ).astype(jnp.bfloat16)
    key_value_columns = key_value_weight.shape[1]
    key_value_start = tp_index * key_value_columns
    key_value_update = lax.dynamic_slice_in_dim(
        key_value_up_factors, key_value_start, key_value_columns, 2
    )[adapter_of_row]
    key_value_low = jnp.where(key_value_start < key_value_width, key_low_rank, value_low_rank)
    kv_part = (
        jnp.dot(normed_input, key_value_weight, preferred_element_type=jnp.float32)
        + jnp.einsum(
            "ep,epg->eg", key_value_low, key_value_update, preferred_element_type=jnp.float32
        )
    ).astype(jnp.bfloat16)
    heads_here = query_part.shape[1] // head_size
    query_group_size = heads_here * tp_count // heads_kv
    key_value_head = tp_index * heads_here // query_group_size
    key_column_count = lax.dynamic_slice_in_dim(
        key_value_up_factors, key_value_head * head_size, head_size, 2
    )[adapter_of_row]
    my_queries = query_part.reshape(row_count, heads_here, head_size)
    factor_part = jnp.einsum(
        "rhd,rjd->rhj", my_queries, key_column_count, preferred_element_type=jnp.float32
    ).astype(jnp.bfloat16)
    factor_part = factor_part.reshape(row_count, heads_here * low_rank_width)
    query_matrix, down_factors, fresh_kv = (
        lax.all_gather(query_part, "tp", axis=1, tiled=True),
        lax.all_gather(factor_part, "tp", axis=1, tiled=True),
        lax.all_gather(kv_part, "tp", axis=1, tiled=True),
    )
    doc_pages = document_page_slots.shape[1]
    owner_of_doc = document_page_slots[:, 0] // doc_pages
    doc_ids = document_of_row[:, 0]
    doc_match = (doc_ids[:, None] == jnp.arange(document_page_slots.shape[0])[None, :]).astype(
        jnp.int32
    )
    target = jnp.sum(doc_match * owner_of_doc[None, :], 1)
    target_match = (target[:, None] == jnp.arange(grp_count)[None, :]).astype(jnp.int32)
    earlier = jnp.cumsum(target_match, 0) - target_match
    capacity = 2 * row_count // grp_count
    slot_of = target * capacity + jnp.sum(earlier * target_match, 1)
    placing = (jnp.arange(grp_count * capacity)[:, None] == slot_of[None, :]).astype(jnp.bfloat16)
    send_queries = (
        jnp.dot(placing, query_matrix, preferred_element_type=jnp.float32)
        .astype(jnp.bfloat16)
        .reshape(grp_count, capacity, -1)
    )
    send_factors = (
        jnp.dot(placing, down_factors, preferred_element_type=jnp.float32)
        .astype(jnp.bfloat16)
        .reshape(grp_count, capacity, -1)
    )
    query_in = lax.all_to_all(send_queries, "grp", split_axis=0, concat_axis=0, tiled=True)
    factor_in = lax.all_to_all(send_factors, "grp", split_axis=0, concat_axis=0, tiled=True)
    per_source = query_in.shape[1]
    item_count = query_in.shape[0] * per_source
    query_flat = query_in.reshape(item_count, -1)
    factor_flat = factor_in.reshape(item_count, -1)
    numerator, factor_sum, maxima, totals = attend_local(
        query_flat,
        factor_flat,
        paged_base_keys,
        paged_base_values,
        paged_down_factors,
        heads_kv,
        low_rank_width,
    )
    all_heads = numerator.shape[1]
    returned = (
        lax.all_to_all(
            numerator.reshape(grp_count, per_source, all_heads, head_size),
            "grp",
            split_axis=0,
            concat_axis=0,
            tiled=True,
        ),
        lax.all_to_all(
            factor_sum.reshape(grp_count, per_source, all_heads, low_rank_width),
            "grp",
            split_axis=0,
            concat_axis=0,
            tiled=True,
        ),
        lax.all_to_all(
            maxima.reshape(grp_count, per_source, all_heads),
            "grp",
            split_axis=0,
            concat_axis=0,
            tiled=True,
        ),
        lax.all_to_all(
            totals.reshape(grp_count, per_source, all_heads),
            "grp",
            split_axis=0,
            concat_axis=0,
            tiled=True,
        ),
    )
    numerator, factor_sum, maxima, totals = [
        piece.reshape((grp_count * capacity,) + piece.shape[2:])[slot_of] for piece in returned
    ]
    numerator, factor_sum, maxima, totals = (
        lax.all_to_all(numerator[:, :, None, :], "tp", split_axis=1, concat_axis=2, tiled=True),
        lax.all_to_all(factor_sum[:, :, None, :], "tp", split_axis=1, concat_axis=2, tiled=True),
        lax.all_to_all(maxima[:, :, None], "tp", split_axis=1, concat_axis=2, tiled=True),
        lax.all_to_all(totals[:, :, None], "tp", split_axis=1, concat_axis=2, tiled=True),
    )
    numerator, factor_sum, maxima, totals = merge_slices(numerator, factor_sum, maxima, totals)
    own_key = lax.dynamic_slice_in_dim(fresh_kv, key_value_head * head_size, head_size, 1)
    value_own = lax.dynamic_slice_in_dim(
        fresh_kv, key_value_width + key_value_head * head_size, head_size, 1
    )
    own_token_score = (
        jnp.einsum("rhd,rd->rh", my_queries, own_key, preferred_element_type=jnp.float32)
        * score_scaling
    )
    peak_all = jnp.maximum(maxima, own_token_score)
    old_scale = jnp.exp(maxima - peak_all)
    own_weight = jnp.exp(own_token_score - peak_all)
    numerator = (
        numerator * old_scale[..., None]
        + own_weight[..., None] * value_own.astype(jnp.float32)[:, None, :]
    )
    factor_sum = factor_sum * old_scale[..., None]
    totals = totals * old_scale + own_weight
    value_column_count = lax.dynamic_slice_in_dim(
        key_value_up_factors, key_value_width + key_value_head * head_size, head_size, 2
    )[adapter_of_row]
    value_shift = jnp.einsum(
        "rhj,rjd->rhd",
        factor_sum,
        value_column_count.astype(jnp.float32),
        precision=lax.Precision.HIGHEST,
    )
    result = ((numerator + value_shift) / totals[..., None]).astype(jnp.bfloat16)
    return result.reshape(row_count, heads_here * head_size)


def solution(mesh):
    in_specs = (
        P("grp", "tp"),
        P(),
        P(None, "tp"),
        P(None, "tp"),
        P(),
        P(None, None, "tp"),
        P(),
        P(("grp", "tp"), None, None),
        P(("grp", "tp"), None, None),
        P(("grp", "tp"), None, None),
        P("grp"),
        P("grp", None),
        P(),
    )
    out_specs = P("grp", "tp")
    fits = mesh.shape["grp"] == 2 and mesh.shape["tp"] == 16
    return jax.shard_map(
        fused_device if fits else per_device, mesh=mesh, in_specs=in_specs, out_specs=out_specs, check_vma=False
    )
```

```python
import functools
import math

import jax
import jax.numpy as jnp
from jax import lax
from jax.experimental import pallas as pl
from jax.experimental.pallas import tpu as pltpu
from jax.sharding import PartitionSpec as P

HEAD_SIZE = 128
MESH = pl.DeviceIdType.MESH
F32 = jnp.float32
BF16 = jnp.bfloat16


def dot(a, b):
    return jnp.dot(a, b, preferred_element_type=F32)


def dot_nt(a, b):
    return lax.dot_general(a, b, (((1,), (1,)), ((), ())), preferred_element_type=F32)


def lanes(shape):
    return lax.broadcasted_iota(jnp.int32, shape, len(shape) - 1)


def split_three(value):
    high = value.astype(BF16).astype(F32)
    middle = (value - high).astype(BF16).astype(F32)
    low = (value - high - middle).astype(BF16).astype(F32)
    return high, middle, low


def fused_kernel(
    x_ref, gain_ref, qw_hbm, kvw_hbm, dn_hbm, qu_hbm, ku_hbm, k_hbm, v_hbm, d_ref,
    adapter_ref, doc_ref, slots_ref, out_ref,
    xbuf, qw, kvw, dn, qu_ref, ku_ref, wo, yq, yo, ssq, kbuf, vbuf, dbuf, qbuf, qcol, kaug, vaug, vup,
    acc, peak, psend, pbuf, fresh, fresh_in,
    load_sem, x_send, x_recv, kv_send, kv_recv, q_send, q_recv, f_send, f_recv, p_send, p_recv,
):
    chunk, rows = x_ref.shape
    width = 16 * chunk
    grp = lax.axis_index("grp")
    tp = lax.axis_index("tp")
    z = tp // 4
    s = tp % 4
    y = s // 2
    c = s % 2
    scale = math.log2(math.e) / math.sqrt(HEAD_SIZE)

    def at(g, t):
        return {"grp": g, "tp": t}

    sibling = at(grp, z * 4 + y * 2 + (1 - c))
    across = at(grp, z * 4 + (1 - y) * 2 + c)
    z_others = [z + 1 - 2 * (z % 2), (z + 2) % 4, 3 - z]

    loads = [
        pltpu.make_async_copy(src, dst, load_sem.at[i])
        for i, (src, dst) in enumerate(
            ((kvw_hbm, kvw), (dn_hbm, dn), (qw_hbm, qw),
             (k_hbm.at[:, :, pl.ds(pl.multiple_of(z * 128, 128), 128)], kbuf.at[z]),
             (v_hbm.at[:, :, pl.ds(pl.multiple_of(z * 128, 128), 128)], vbuf.at[z]),
             (qu_hbm, qu_ref), (ku_hbm, ku_ref))
        )
    ]
    for load in loads:
        load.start()

    barrier = pltpu.get_barrier_semaphore()
    for i in range(1, 16):
        pl.semaphore_signal(barrier, inc=1, device_id=at(grp, (tp + i) % 16), device_id_type=MESH)
    for j in range(4):
        pl.semaphore_signal(barrier, inc=1, device_id=at(1 - grp, z * 4 + j), device_id_type=MESH)
    dbuf[z] = d_ref[...].reshape(128, 128)
    gain = jnp.zeros((1, chunk), F32)
    for t in range(16):
        gain = gain + jnp.where(tp == t, gain_ref[:, t * chunk : (t + 1) * chunk], 0.0)
    x_rows = x_ref[...].T.astype(F32)
    pieces = split_three(jnp.sum(x_rows * x_rows, axis=-1, keepdims=True))
    xbuf[tp, :, :chunk] = (x_rows * gain).astype(BF16)
    spare = lanes((rows, 384 - chunk))
    sums = jnp.zeros(spare.shape, F32)
    for i, piece in enumerate(pieces):
        sums = jnp.where(spare == i, piece, sums)
    xbuf[tp, :, chunk:] = sums.astype(BF16)
    pl.semaphore_wait(barrier, 19)

    started = []

    def send(src, dst, send_sem, recv_sem, device):
        copy = pltpu.make_async_remote_copy(
            src_ref=src, dst_ref=dst, send_sem=send_sem, recv_sem=recv_sem,
            device_id=device, device_id_type=MESH,
        )
        copy.start()
        return copy

    def arrive(dst, send_sem, recv_sem):
        pltpu.make_async_remote_copy(
            src_ref=dst, dst_ref=dst, send_sem=send_sem, recv_sem=recv_sem,
            device_id=sibling, device_id_type=MESH,
        ).wait_recv()

    def send_x(t, sem, device):
        copy = send(xbuf.at[t], xbuf.at[t], x_send.at[sem], x_recv.at[t], device)
        started.append(copy)
        return copy

    def send_q(index, sem, device):
        started.append(send(qbuf.at[index], qbuf.at[index], q_send.at[sem], q_recv.at[index], device))

    send_x(tp, 0, at(grp, z_others[1] * 4 + s))
    send_x(tp, 1, at(grp, z_others[0] * 4 + s))
    send_x(tp, 3, across)
    send_x(tp, 7, sibling)
    def send_kv(i):
        zo = z_others[i]
        cols = pl.ds(pl.multiple_of(zo * 128, 128), 128)
        for n, (src, dst) in enumerate(
            ((k_hbm.at[:, :, cols], kbuf), (v_hbm.at[:, :, cols], vbuf), (dbuf.at[z], dbuf))
        ):
            started.append(
                send(src, dst.at[z], kv_send.at[i * 3 + n], kv_recv.at[z * 3 + n], at(grp, zo * 4 + s))
            )

    loads[0].wait()
    loads[1].wait()

    def join(i, carry):
        part = pl.ds(pl.multiple_of(i * 128, 128), 128)
        both = jnp.concatenate([kvw[:, part], dn[:, part], jnp.zeros((16, 128), BF16)], axis=0)
        wo[part, :] = both.T
        return carry

    lax.fori_loop(0, width // 128, join, 0)
    yq[...] = jnp.zeros_like(yq)
    yo[...] = jnp.zeros_like(yo)
    ssq[...] = jnp.zeros_like(ssq)
    loads[2].wait()

    def project(t):
        scaled = xbuf[t, :, :chunk]
        ssq[...] += jnp.sum(xbuf[t, :, chunk:].astype(F32), axis=-1, keepdims=True)
        part = pl.ds(pl.multiple_of(t * chunk, 64), chunk)
        yq[...] += dot(scaled, qw[part, :])
        yo[...] += dot(scaled, wo[part, :])

    def augment(zo):
        down = dbuf[zo].astype(F32).T.astype(BF16)
        for p in range(4):
            part = pl.ds(p * 128, 128)
            kaug[zo, part, :128] = kbuf[zo, p]
            kaug[zo, part, 128:] = jnp.concatenate(
                [down[:, p * 32 : p * 32 + 16], jnp.zeros((128, 112), BF16)], axis=1
            )
            vaug[zo, :128, part] = vbuf[zo, p].T
            vaug[zo, 128:144, part] = dbuf[zo, p * 32 + 16 : p * 32 + 32, :]
        first_row = lax.broadcasted_iota(jnp.int32, (16, 512), 0) == 0
        vaug[zo, 144:, :] = first_row.astype(F32).astype(BF16)

    def attend(zo, j, start):
        scores = dot(kaug[zo], qcol[j])
        top = jnp.max(scores, axis=0, keepdims=True) * scale
        if not start:
            old = peak[j]
            top = jnp.maximum(old, top)
        weights = jnp.exp2(scores * scale - top).astype(BF16)
        product = dot(vaug[zo], weights)
        if start:
            acc[j] = product
        else:
            acc[j] = acc[j] * jnp.exp2(old - top) + product
        peak[j] = top

    project(tp)
    loads[3].wait()
    loads[4].wait()
    loads[5].wait()
    loads[6].wait()
    augment(z)
    qcol[:, 144:, :] = jnp.zeros((4, 112, 512), BF16)
    vup[...] = (
        ku_ref[:, :, pl.ds(pl.multiple_of(512 + z * 128, 128), 128)].reshape(256, 128).T
    )
    for i in (1, 0, 2):
        t = z_others[i] * 4 + s
        arrive(xbuf.at[t], x_send.at[0], x_recv.at[t])
        if i == 1:
            send_x(t, 2, at(grp, z_others[0] * 4 + s))
        send_x(t, 4 + i, across)
        send_x(t, 8 + i, sibling)
    send_kv(1)
    send_kv(2)
    for i in (1, 0, 2):
        project(z_others[i] * 4 + s)
    for i, zo in enumerate([z] + z_others):
        t = zo * 4 + (1 - y) * 2 + c
        arrive(xbuf.at[t], x_send.at[0], x_recv.at[t])
        send_x(t, 11 + i, sibling)
        project(t)
    for zo in [z] + z_others:
        for yo_ in (y, 1 - y):
            t = zo * 4 + yo_ * 2 + (1 - c)
            arrive(xbuf.at[t], x_send.at[0], x_recv.at[t])
            project(t)

    rinv = lax.rsqrt(ssq[...] * (1.0 / width) + 1e-06)
    other = yo[...] * rinv
    low = other[:, 64:128].astype(BF16)
    def column(row_ref):
        return jnp.broadcast_to(row_ref[...].astype(F32), (rows, rows)).T.astype(jnp.int32)

    adapter = column(adapter_ref)
    adapter = jnp.concatenate([adapter, adapter], axis=1)
    wide = lanes((rows, 256))
    picked = (wide // 16) == adapter
    row_of = lax.broadcasted_iota(jnp.int32, (64, 256), 0)
    col_of = lanes((64, 256)) % 16

    def spread(part, offset):
        tile = (row_of == col_of + offset).astype(F32).astype(BF16)
        return jnp.where(picked, dot(part, tile), 0.0).astype(BF16)

    queries = (yq[...] * rinv + dot(spread(low, 0), qu_ref[...].reshape(256, 256))).astype(BF16)
    odd = tp % 2
    is_key = tp < 8
    kv_low = jnp.where(is_key, spread(low, 16).astype(F32), spread(low, 32).astype(F32)).astype(BF16)
    pair_cols = pl.ds(pl.multiple_of((tp // 2) * 128, 128), 128)
    kv_update = dot(kv_low, ku_ref[:, :, pair_cols].reshape(256, 128))
    kv_base = other[:, :64]
    kv_full = (jnp.concatenate([kv_base, kv_base], axis=1) + kv_update).T
    fresh[...] = jnp.where(odd == 1, kv_full[64:], kv_full[:64]).astype(BF16)
    fold_row = lax.broadcasted_iota(jnp.int32, (256, 128), 0) % 16
    fold_col = lanes((256, 128))
    key_up = ku_ref[:, :, pl.ds(pl.multiple_of(z * 128, 128), 128)].reshape(256, 128)
    factors = jnp.zeros((rows, 128), F32)
    for h in range(2):
        full = dot_nt(queries[:, h * 128 : (h + 1) * 128], key_up)
        full = jnp.where(picked, full, 0.0).astype(BF16)
        fold = (fold_col == fold_row + 16 * h).astype(F32).astype(BF16)
        factors = factors + dot(full, fold)
    mine = 4 * grp + s
    qbuf[mine, :256, :] = queries.astype(F32).T.astype(BF16)
    qbuf[mine, 256:, :] = factors.T[:32].astype(BF16)

    far = (1 - y) * 2 + c
    direct = [(grp, far), (1 - grp, s), (1 - grp, far)]
    for n, (g, j) in enumerate(direct):
        send_q(mine, n, at(g, z * 4 + j))
    send_q(mine, 3, sibling)
    head = (tp % 8) // 2
    slot = (tp // 8) * 2 + odd
    for j in range(4):
        target = head * 4 + j

        @pl.when(target != tp)
        def _():
            send(fresh, fresh_in.at[slot], f_send.at[j], f_recv.at[slot], at(grp, target))

        @pl.when(target == tp)
        def _():
            fresh_in[slot] = fresh[...]

    send_kv(0)
    for n, (g, j) in enumerate(direct):
        index = 4 * g + j
        arrive(qbuf.at[index], x_send.at[0], q_recv.at[index])
        send_q(index, 4 + n, sibling)
    for j, waited in ((s, True), (far, True), (y * 2 + 1 - c, False), (3 - s, False)):
        for g in (grp, 1 - grp):
            index = 4 * g + j
            if not waited:
                arrive(qbuf.at[index], x_send.at[0], q_recv.at[index])
            for h in range(2):
                part = pl.ds(pl.multiple_of(h * 256 + g * 128, 128), 128)
                qcol[j, :128, part] = qbuf[index, h * 128 : (h + 1) * 128, :]
                qcol[j, 128:144, part] = qbuf[index, 256 + h * 16 : 272 + h * 16, :]
        attend(z, j, True)

    def arrived(zo):
        for n2, dst in enumerate((kbuf, vbuf, dbuf)):
            arrive(dst.at[zo], x_send.at[0], kv_recv.at[zo * 3 + n2])

    for zo in z_others[1:]:
        arrived(zo)
        augment(zo)

        def body(j, carry):
            attend(zo, j, False)
            return carry

        lax.fori_loop(0, 4, body, 0)

    arrived(z_others[0])
    augment(z_others[0])

    def last(shift, carry):
        j = (s + shift) % 4
        attend(z_others[0], j, False)
        line = lax.broadcasted_iota(jnp.int32, (16, 128), 0)
        for g in range(2):
            for h in range(2):
                part = pl.ds(h * 256 + g * 128, 128)
                psend[j, g, h * 128 : (h + 1) * 128, :] = acc[j, :128, part].astype(BF16)
                psend[j, g, 256 + h * 32 : 272 + h * 32, :] = acc[j, 128:144, part].astype(BF16)
                stats = jnp.zeros((16, 128), F32)
                pieces = split_three(acc[j, 144:145, part])[:2] + split_three(peak[j, :, part])
                for i, piece in enumerate(pieces):
                    stats = jnp.where(line == i, piece, stats)
                psend[j, g, 272 + h * 32 : 288 + h * 32, :] = stats.astype(BF16)
            here = jnp.logical_and(j == s, grp == g)

            @pl.when(jnp.logical_not(here))
            def _():
                send(psend.at[j, g], pbuf.at[mine], p_send.at[j * 2 + g], p_recv.at[mine], at(g, z * 4 + j))

            @pl.when(here)
            def _():
                pbuf[mine] = psend[j, g]

        return carry

    lax.fori_loop(1, 5, last, 0)

    for n in range(4):
        source = (n // 2) * 8 + 2 * z + n % 2

        @pl.when(source != tp)
        def _():
            arrive(fresh_in.at[n], x_send.at[0], f_recv.at[n])

    own_key = jnp.concatenate([fresh_in[0], fresh_in[1]], axis=0).astype(F32)
    own_value = jnp.concatenate([fresh_in[2], fresh_in[3]], axis=0).astype(F32)
    for n in range(1, 8):
        index = (mine + n) % 8
        arrive(pbuf.at[index], x_send.at[0], p_recv.at[index])
    half = slots_ref.shape[1]
    holder = jnp.where(doc_ref[...] == 0, slots_ref[0, 0] // half, slots_ref[1, 0] // half)
    picked = lax.broadcasted_iota(jnp.int32, (256, rows), 0) // 16 == adapter_ref[...]
    blocks = [
        jnp.where(holder == 0, pbuf[j].astype(F32), pbuf[4 + j].astype(F32)) for j in range(4)
    ]
    for h in range(2):
        query = qbuf[mine, h * 128 : (h + 1) * 128, :].astype(F32)
        own = jnp.sum(query * own_key, axis=0, keepdims=True) * scale
        base = 256 + h * 32
        peaks = [b[base + 18 : base + 19] + b[base + 19 : base + 20] + b[base + 20 : base + 21] for b in blocks]
        top = own
        for m in peaks:
            top = jnp.maximum(top, m)
        total = jnp.exp2(own - top)
        numerator = total * own_value
        factor = jnp.zeros((16, rows), F32)
        for block, m in zip(blocks, peaks):
            weight = jnp.exp2(m - top)
            numerator = numerator + block[h * 128 : (h + 1) * 128] * weight
            factor = factor + block[base : base + 16] * weight
            total = total + (block[base + 16 : base + 17] + block[base + 17 : base + 18]) * weight
        expanded = jnp.where(picked, jnp.concatenate([factor] * 16, axis=0), 0.0)
        high = expanded.astype(BF16)
        shift = dot(vup[...], high) + dot(vup[...], (expanded - high.astype(F32)).astype(BF16))
        out_ref[:, h * 128 : (h + 1) * 128] = ((numerator + shift) / total).T.astype(BF16)

    for copy in started:
        copy.wait_send()
    for j in range(4):
        target = head * 4 + j

        @pl.when(target != tp)
        def _():
            pltpu.make_async_remote_copy(
                src_ref=fresh, dst_ref=fresh_in.at[slot], send_sem=f_send.at[j],
                recv_sem=f_recv.at[slot], device_id=at(grp, target), device_id_type=MESH,
            ).wait_send()

    for j in range(4):
        for g in range(2):

            @pl.when(jnp.logical_not(jnp.logical_and(j == s, grp == g)))
            def _():
                pltpu.make_async_remote_copy(
                    src_ref=psend.at[j, g], dst_ref=pbuf.at[mine], send_sem=p_send.at[j * 2 + g],
                    recv_sem=p_recv.at[mine], device_id=at(g, z * 4 + j), device_id_type=MESH,
                ).wait_send()


def fused_device(
    residual_input, input_norm_gain, query_weight, key_value_weight, shared_down_factors,
    query_up_factors, key_value_up_factors, paged_base_keys, paged_base_values,
    paged_down_factors, adapter_of_row, document_of_row, document_page_slots,
):
    rows, chunk = residual_input.shape
    vmem = pl.BlockSpec(memory_space=pltpu.VMEM)
    hbm = pl.BlockSpec(memory_space=pltpu.HBM)
    smem = pl.BlockSpec(memory_space=pltpu.SMEM)
    dma = pltpu.SemaphoreType.DMA
    width = 16 * chunk
    return pl.pallas_call(
        fused_kernel,
        out_shape=jax.ShapeDtypeStruct((rows, 256), BF16),
        in_specs=[vmem, vmem, hbm, hbm, hbm, hbm, hbm, hbm, hbm, vmem, vmem, vmem, smem],
        out_specs=vmem,
        scratch_shapes=[
            pltpu.VMEM((16, rows, 384), BF16),
            pltpu.VMEM((width, 256), BF16),
            pltpu.VMEM((64, width), BF16),
            pltpu.VMEM((48, width), BF16),
            pltpu.VMEM((16, 16, 256), BF16),
            pltpu.VMEM((16, 16, 1024), BF16),
            pltpu.VMEM((width, 128), BF16),
            pltpu.VMEM((rows, 256), F32),
            pltpu.VMEM((rows, 128), F32),
            pltpu.VMEM((rows, 1), F32),
            pltpu.VMEM((4, 4, 128, 128), BF16),
            pltpu.VMEM((4, 4, 128, 128), BF16),
            pltpu.VMEM((4, 128, 128), BF16),
            pltpu.VMEM((8, 288, rows), BF16),
            pltpu.VMEM((4, 256, 4 * rows), BF16),
            pltpu.VMEM((4, 512, 256), BF16),
            pltpu.VMEM((4, 160, 512), BF16),
            pltpu.VMEM((128, 256), BF16),
            pltpu.VMEM((4, 160, 4 * rows), F32),
            pltpu.VMEM((4, 1, 4 * rows), F32),
            pltpu.VMEM((4, 2, 320, rows), BF16),
            pltpu.VMEM((8, 320, rows), BF16),
            pltpu.VMEM((64, rows), BF16),
            pltpu.VMEM((4, 64, rows), BF16),
            dma((7,)), dma((16,)), dma((16,)), dma((9,)), dma((12,)),
            dma((7,)), dma((8,)), dma((4,)), dma((4,)), dma((8,)), dma((8,)),
        ],
        compiler_params=pltpu.CompilerParams(
            collective_id=0, has_side_effects=True, vmem_limit_bytes=63 * 1024 * 1024
        ),
        cost_estimate=pl.CostEstimate(
            flops=5_000_000_000, bytes_accessed=8_000_000, transcendentals=4_500_000
        ),
    )(
        residual_input.T, input_norm_gain.reshape(1, width), query_weight, key_value_weight.T,
        shared_down_factors.T, query_up_factors, key_value_up_factors, paged_base_keys,
        paged_base_values, paged_down_factors.transpose(0, 2, 1), adapter_of_row.reshape(1, rows),
        document_of_row.reshape(1, rows), document_page_slots,
    )


def merge_slices(numerator, factor_sum, maxima, totals):
    peak_all = jnp.max(maxima, axis=-1)
    weight = jnp.exp(maxima - peak_all[..., None])
    numerator = jnp.sum(numerator * weight[..., None], axis=-2)
    factor_sum = jnp.sum(factor_sum * weight[..., None], axis=-2)
    totals = jnp.sum(totals * weight, axis=-1)
    return (numerator, factor_sum, peak_all, totals)


def attend_local(
    query_matrix,
    down_factors,
    paged_base_keys,
    paged_base_values,
    paged_down_factors,
    heads_kv,
    low_rank_width,
):
    item_count = query_matrix.shape[0]
    head_size = paged_base_keys.shape[-1] // heads_kv
    all_heads = query_matrix.shape[1] // head_size
    query_group_size = all_heads // heads_kv
    local_tokens = paged_base_keys.shape[0] * paged_base_keys.shape[1]
    score_scaling = head_size ** (-0.5)
    key_heads = paged_base_keys.reshape(local_tokens, heads_kv, head_size).transpose(1, 0, 2)
    value_heads = paged_base_values.reshape(local_tokens, heads_kv, head_size).transpose(1, 0, 2)
    factor_flat = paged_down_factors.reshape(local_tokens, 2 * low_rank_width)
    cached_key = factor_flat[:, :low_rank_width]
    cached_value = factor_flat[:, low_rank_width:]
    query_head_count = query_matrix.reshape(
        item_count, heads_kv, query_group_size, head_size
    ).transpose(1, 0, 2, 3)
    factor_heads = down_factors.reshape(
        item_count, heads_kv, query_group_size, low_rank_width
    ).transpose(1, 0, 2, 3)

    def one_head(bundle):
        query_one, factor_one, key_one, value_one = bundle
        scores = (
            jnp.einsum("ngd,ld->ngl", query_one, key_one, preferred_element_type=jnp.float32)
            + jnp.einsum("ngj,lj->ngl", factor_one, cached_key, preferred_element_type=jnp.float32)
        ) * score_scaling
        maxima = jnp.max(scores, -1)
        weights = jnp.exp(scores - maxima[..., None])
        totals = jnp.sum(weights, -1)
        rounded = weights.astype(jnp.bfloat16)
        numerator = jnp.einsum(
            "ngl,ld->ngd", rounded, value_one, preferred_element_type=jnp.float32
        )
        factor_sum = jnp.einsum(
            "ngl,lj->ngj", rounded, cached_value, preferred_element_type=jnp.float32
        )
        return (numerator, factor_sum, maxima, totals)

    numerator, factor_sum, maxima, totals = lax.map(
        one_head, (query_head_count, factor_heads, key_heads, value_heads)
    )
    numerator = numerator.transpose(1, 0, 2, 3).reshape(item_count, all_heads, head_size)
    factor_sum = factor_sum.transpose(1, 0, 2, 3).reshape(item_count, all_heads, low_rank_width)
    maxima = maxima.transpose(1, 0, 2).reshape(item_count, all_heads)
    totals = totals.transpose(1, 0, 2).reshape(item_count, all_heads)
    return (numerator, factor_sum, maxima, totals)


def per_device(
    residual_input,
    input_norm_gain,
    query_weight,
    key_value_weight,
    shared_down_factors,
    query_up_factors,
    key_value_up_factors,
    paged_base_keys,
    paged_base_values,
    paged_down_factors,
    adapter_of_row,
    document_of_row,
    document_page_slots,
):
    tp_count = lax.axis_size("tp")
    grp_count = lax.axis_size("grp")
    tp_index = lax.axis_index("tp")
    low_rank_width = shared_down_factors.shape[1] // 3
    key_value_width = key_value_up_factors.shape[2] // 2
    head_size = HEAD_SIZE
    heads_kv = key_value_width // head_size
    row_count = residual_input.shape[0]
    score_scaling = head_size ** (-0.5)
    gathered = lax.all_gather(residual_input, "tp", axis=1, tiled=True).astype(jnp.float32)
    normed_input = (
        gathered
        * lax.rsqrt(jnp.mean(gathered * gathered, -1, keepdims=True) + 1e-06)
        * input_norm_gain
    ).astype(jnp.bfloat16)
    low_rank_part = jnp.dot(
        normed_input, shared_down_factors, preferred_element_type=jnp.float32
    ).astype(jnp.bfloat16)
    query_low_rank = low_rank_part[:, :low_rank_width]
    key_low_rank = low_rank_part[:, low_rank_width : 2 * low_rank_width]
    value_low_rank = low_rank_part[:, 2 * low_rank_width :]
    query_update = query_up_factors[adapter_of_row]
    query_part = (
        jnp.dot(normed_input, query_weight, preferred_element_type=jnp.float32)
        + jnp.einsum("ep,epg->eg", query_low_rank, query_update, preferred_element_type=jnp.float32)
    ).astype(jnp.bfloat16)
    key_value_columns = key_value_weight.shape[1]
    key_value_start = tp_index * key_value_columns
    key_value_update = lax.dynamic_slice_in_dim(
        key_value_up_factors, key_value_start, key_value_columns, 2
    )[adapter_of_row]
    key_value_low = jnp.where(key_value_start < key_value_width, key_low_rank, value_low_rank)
    kv_part = (
        jnp.dot(normed_input, key_value_weight, preferred_element_type=jnp.float32)
        + jnp.einsum(
            "ep,epg->eg", key_value_low, key_value_update, preferred_element_type=jnp.float32
        )
    ).astype(jnp.bfloat16)
    heads_here = query_part.shape[1] // head_size
    query_group_size = heads_here * tp_count // heads_kv
    key_value_head = tp_index * heads_here // query_group_size
    key_column_count = lax.dynamic_slice_in_dim(
        key_value_up_factors, key_value_head * head_size, head_size, 2
    )[adapter_of_row]
    my_queries = query_part.reshape(row_count, heads_here, head_size)
    factor_part = jnp.einsum(
        "rhd,rjd->rhj", my_queries, key_column_count, preferred_element_type=jnp.float32
    ).astype(jnp.bfloat16)
    factor_part = factor_part.reshape(row_count, heads_here * low_rank_width)
    query_matrix, down_factors, fresh_kv = (
        lax.all_gather(query_part, "tp", axis=1, tiled=True),
        lax.all_gather(factor_part, "tp", axis=1, tiled=True),
        lax.all_gather(kv_part, "tp", axis=1, tiled=True),
    )
    doc_pages = document_page_slots.shape[1]
    owner_of_doc = document_page_slots[:, 0] // doc_pages
    doc_ids = document_of_row[:, 0]
    doc_match = (doc_ids[:, None] == jnp.arange(document_page_slots.shape[0])[None, :]).astype(
        jnp.int32
    )
    target = jnp.sum(doc_match * owner_of_doc[None, :], 1)
    target_match = (target[:, None] == jnp.arange(grp_count)[None, :]).astype(jnp.int32)
    earlier = jnp.cumsum(target_match, 0) - target_match
    capacity = 2 * row_count // grp_count
    slot_of = target * capacity + jnp.sum(earlier * target_match, 1)
    placing = (jnp.arange(grp_count * capacity)[:, None] == slot_of[None, :]).astype(jnp.bfloat16)
    send_queries = (
        jnp.dot(placing, query_matrix, preferred_element_type=jnp.float32)
        .astype(jnp.bfloat16)
        .reshape(grp_count, capacity, -1)
    )
    send_factors = (
        jnp.dot(placing, down_factors, preferred_element_type=jnp.float32)
        .astype(jnp.bfloat16)
        .reshape(grp_count, capacity, -1)
    )
    query_in = lax.all_to_all(send_queries, "grp", split_axis=0, concat_axis=0, tiled=True)
    factor_in = lax.all_to_all(send_factors, "grp", split_axis=0, concat_axis=0, tiled=True)
    per_source = query_in.shape[1]
    item_count = query_in.shape[0] * per_source
    query_flat = query_in.reshape(item_count, -1)
    factor_flat = factor_in.reshape(item_count, -1)
    numerator, factor_sum, maxima, totals = attend_local(
        query_flat,
        factor_flat,
        paged_base_keys,
        paged_base_values,
        paged_down_factors,
        heads_kv,
        low_rank_width,
    )
    all_heads = numerator.shape[1]
    returned = (
        lax.all_to_all(
            numerator.reshape(grp_count, per_source, all_heads, head_size),
            "grp",
            split_axis=0,
            concat_axis=0,
            tiled=True,
        ),
        lax.all_to_all(
            factor_sum.reshape(grp_count, per_source, all_heads, low_rank_width),
            "grp",
            split_axis=0,
            concat_axis=0,
            tiled=True,
        ),
        lax.all_to_all(
            maxima.reshape(grp_count, per_source, all_heads),
            "grp",
            split_axis=0,
            concat_axis=0,
            tiled=True,
        ),
        lax.all_to_all(
            totals.reshape(grp_count, per_source, all_heads),
            "grp",
            split_axis=0,
            concat_axis=0,
            tiled=True,
        ),
    )
    numerator, factor_sum, maxima, totals = [
        piece.reshape((grp_count * capacity,) + piece.shape[2:])[slot_of] for piece in returned
    ]
    numerator, factor_sum, maxima, totals = (
        lax.all_to_all(numerator[:, :, None, :], "tp", split_axis=1, concat_axis=2, tiled=True),
        lax.all_to_all(factor_sum[:, :, None, :], "tp", split_axis=1, concat_axis=2, tiled=True),
        lax.all_to_all(maxima[:, :, None], "tp", split_axis=1, concat_axis=2, tiled=True),
        lax.all_to_all(totals[:, :, None], "tp", split_axis=1, concat_axis=2, tiled=True),
    )
    numerator, factor_sum, maxima, totals = merge_slices(numerator, factor_sum, maxima, totals)
    own_key = lax.dynamic_slice_in_dim(fresh_kv, key_value_head * head_size, head_size, 1)
    value_own = lax.dynamic_slice_in_dim(
        fresh_kv, key_value_width + key_value_head * head_size, head_size, 1
    )
    own_token_score = (
        jnp.einsum("rhd,rd->rh", my_queries, own_key, preferred_element_type=jnp.float32)
        * score_scaling
    )
    peak_all = jnp.maximum(maxima, own_token_score)
    old_scale = jnp.exp(maxima - peak_all)
    own_weight = jnp.exp(own_token_score - peak_all)
    numerator = (
        numerator * old_scale[..., None]
        + own_weight[..., None] * value_own.astype(jnp.float32)[:, None, :]
    )
    factor_sum = factor_sum * old_scale[..., None]
    totals = totals * old_scale + own_weight
    value_column_count = lax.dynamic_slice_in_dim(
        key_value_up_factors, key_value_width + key_value_head * head_size, head_size, 2
    )[adapter_of_row]
    value_shift = jnp.einsum(
        "rhj,rjd->rhd",
        factor_sum,
        value_column_count.astype(jnp.float32),
        precision=lax.Precision.HIGHEST,
    )
    result = ((numerator + value_shift) / totals[..., None]).astype(jnp.bfloat16)
    return result.reshape(row_count, heads_here * head_size)


def solution(mesh):
    in_specs = (
        P("grp", "tp"),
        P(),
        P(None, "tp"),
        P(None, "tp"),
        P(),
        P(None, None, "tp"),
        P(),
        P(("grp", "tp"), None, None),
        P(("grp", "tp"), None, None),
        P(("grp", "tp"), None, None),
        P("grp"),
        P("grp", None),
        P(),
    )
    out_specs = P("grp", "tp")
    fits = mesh.shape["grp"] == 2 and mesh.shape["tp"] == 16
    return jax.shard_map(
        fused_device if fits else per_device, mesh=mesh, in_specs=in_specs, out_specs=out_specs, check_vma=False
    )
```

```python
import functools
import math

import jax
import jax.numpy as jnp
from jax import lax
from jax.experimental import pallas as pl
from jax.experimental.pallas import tpu as pltpu
from jax.sharding import PartitionSpec as P

HEAD_SIZE = 128
MESH = pl.DeviceIdType.MESH
F32 = jnp.float32
BF16 = jnp.bfloat16


def dot(a, b):
    return jnp.dot(a, b, preferred_element_type=F32)


def dot_nt(a, b):
    return lax.dot_general(a, b, (((1,), (1,)), ((), ())), preferred_element_type=F32)


def lanes(shape):
    return lax.broadcasted_iota(jnp.int32, shape, len(shape) - 1)


def split_three(value):
    high = value.astype(BF16).astype(F32)
    middle = (value - high).astype(BF16).astype(F32)
    low = (value - high - middle).astype(BF16).astype(F32)
    return high, middle, low


def fused_kernel(
    x_ref, gain_ref, qw_hbm, kvw_hbm, dn_hbm, qu_hbm, ku_hbm, k_hbm, v_hbm, d_ref,
    adapter_ref, doc_ref, slots_ref, out_ref,
    xbuf, qw, kvw, dn, qu_ref, ku_ref, wo, yq, yo, ssq, kbuf, vbuf, dbuf, qbuf, qcol, kaug, vaug, vup,
    acc, peak, psend, pbuf, fresh, fresh_in,
    load_sem, x_send, x_recv, kv_send, kv_recv, q_send, q_recv, f_send, f_recv, p_send, p_recv,
):
    chunk, rows = x_ref.shape
    width = 16 * chunk
    grp = lax.axis_index("grp")
    tp = lax.axis_index("tp")
    z = tp // 4
    s = tp % 4
    y = s // 2
    c = s % 2
    scale = math.log2(math.e) / math.sqrt(HEAD_SIZE)

    def at(g, t):
        return {"grp": g, "tp": t}

    sibling = at(grp, z * 4 + y * 2 + (1 - c))
    across = at(grp, z * 4 + (1 - y) * 2 + c)
    z_others = [z + 1 - 2 * (z % 2), (z + 2) % 4, 3 - z]

    loads = [
        pltpu.make_async_copy(src, dst, load_sem.at[i])
        for i, (src, dst) in enumerate(
            ((kvw_hbm, kvw), (dn_hbm, dn), (qw_hbm, qw),
             (k_hbm.at[:, :, pl.ds(pl.multiple_of(z * 128, 128), 128)], kbuf.at[z]),
             (v_hbm.at[:, :, pl.ds(pl.multiple_of(z * 128, 128), 128)], vbuf.at[z]),
             (qu_hbm, qu_ref), (ku_hbm, ku_ref))
        )
    ]
    for load in loads:
        load.start()

    barrier = pltpu.get_barrier_semaphore()
    for i in range(1, 16):
        pl.semaphore_signal(barrier, inc=1, device_id=at(grp, (tp + i) % 16), device_id_type=MESH)
    for j in range(4):
        pl.semaphore_signal(barrier, inc=1, device_id=at(1 - grp, z * 4 + j), device_id_type=MESH)
    dbuf[z] = d_ref[...].reshape(128, 128)
    gain = jnp.zeros((1, chunk), F32)
    for t in range(16):
        gain = gain + jnp.where(tp == t, gain_ref[:, t * chunk : (t + 1) * chunk], 0.0)
    x_rows = x_ref[...].T.astype(F32)
    pieces = split_three(jnp.sum(x_rows * x_rows, axis=-1, keepdims=True))
    xbuf[tp, :, :chunk] = (x_rows * gain).astype(BF16)
    spare = lanes((rows, 384 - chunk))
    sums = jnp.zeros(spare.shape, F32)
    for i, piece in enumerate(pieces):
        sums = jnp.where(spare == i, piece, sums)
    xbuf[tp, :, chunk:] = sums.astype(BF16)
    pl.semaphore_wait(barrier, 19)

    started = []

    def send(src, dst, send_sem, recv_sem, device):
        copy = pltpu.make_async_remote_copy(
            src_ref=src, dst_ref=dst, send_sem=send_sem, recv_sem=recv_sem,
            device_id=device, device_id_type=MESH,
        )
        copy.start()
        return copy

    def arrive(dst, send_sem, recv_sem):
        pltpu.make_async_remote_copy(
            src_ref=dst, dst_ref=dst, send_sem=send_sem, recv_sem=recv_sem,
            device_id=sibling, device_id_type=MESH,
        ).wait_recv()

    def send_x(t, sem, device):
        copy = send(xbuf.at[t], xbuf.at[t], x_send.at[sem], x_recv.at[t], device)
        started.append(copy)
        return copy

    def send_q(index, sem, device):
        started.append(send(qbuf.at[index], qbuf.at[index], q_send.at[sem], q_recv.at[index], device))

    send_x(tp, 0, at(grp, z_others[1] * 4 + s))
    send_x(tp, 1, at(grp, z_others[0] * 4 + s))
    send_x(tp, 3, across)
    send_x(tp, 7, sibling)
    def send_kv(i):
        zo = z_others[i]
        cols = pl.ds(pl.multiple_of(zo * 128, 128), 128)
        for n, (src, dst) in enumerate(
            ((k_hbm.at[:, :, cols], kbuf), (v_hbm.at[:, :, cols], vbuf), (dbuf.at[z], dbuf))
        ):
            started.append(
                send(src, dst.at[z], kv_send.at[i * 3 + n], kv_recv.at[z * 3 + n], at(grp, zo * 4 + s))
            )

    loads[0].wait()
    loads[1].wait()

    def join(i, carry):
        part = pl.ds(pl.multiple_of(i * 128, 128), 128)
        both = jnp.concatenate([kvw[:, part], dn[:, part], jnp.zeros((16, 128), BF16)], axis=0)
        wo[part, :] = both.T
        return carry

    lax.fori_loop(0, width // 128, join, 0)
    yq[...] = jnp.zeros_like(yq)
    yo[...] = jnp.zeros_like(yo)
    ssq[...] = jnp.zeros_like(ssq)
    loads[2].wait()

    def project(t):
        scaled = xbuf[t, :, :chunk]
        ssq[...] += jnp.sum(xbuf[t, :, chunk:].astype(F32), axis=-1, keepdims=True)
        part = pl.ds(pl.multiple_of(t * chunk, 64), chunk)
        yq[...] += dot(scaled, qw[part, :])
        yo[...] += dot(scaled, wo[part, :])

    def augment(zo):
        down = dbuf[zo].astype(F32).T.astype(BF16)
        for p in range(4):
            part = pl.ds(p * 128, 128)
            kaug[zo, part, :128] = kbuf[zo, p]
            kaug[zo, part, 128:] = jnp.concatenate(
                [down[:, p * 32 : p * 32 + 16], jnp.zeros((128, 112), BF16)], axis=1
            )
            vaug[zo, :128, part] = vbuf[zo, p].T
            vaug[zo, 128:144, part] = dbuf[zo, p * 32 + 16 : p * 32 + 32, :]
        first_row = lax.broadcasted_iota(jnp.int32, (16, 512), 0) == 0
        vaug[zo, 144:, :] = first_row.astype(F32).astype(BF16)

    def attend(zo, j, start):
        scores = dot(kaug[zo], qcol[j])
        top = jnp.max(scores, axis=0, keepdims=True) * scale
        if not start:
            old = peak[j]
            top = jnp.maximum(old, top)
        weights = jnp.exp2(scores * scale - top).astype(BF16)
        product = dot(vaug[zo], weights)
        if start:
            acc[j] = product
        else:
            acc[j] = acc[j] * jnp.exp2(old - top) + product
        peak[j] = top

    project(tp)
    loads[3].wait()
    loads[4].wait()
    loads[5].wait()
    loads[6].wait()
    augment(z)
    qcol[:, 144:, :] = jnp.zeros((4, 112, 512), BF16)
    vup[...] = (
        ku_ref[:, :, pl.ds(pl.multiple_of(512 + z * 128, 128), 128)].reshape(256, 128).T
    )
    for i in (1, 0, 2):
        t = z_others[i] * 4 + s
        arrive(xbuf.at[t], x_send.at[0], x_recv.at[t])
        if i == 1:
            send_x(t, 2, at(grp, z_others[0] * 4 + s))
        send_x(t, 4 + i, across)
        send_x(t, 8 + i, sibling)
    send_kv(1)
    send_kv(0)
    for i in (1, 0, 2):
        project(z_others[i] * 4 + s)
    for i, zo in enumerate([z] + z_others):
        t = zo * 4 + (1 - y) * 2 + c
        arrive(xbuf.at[t], x_send.at[0], x_recv.at[t])
        send_x(t, 11 + i, sibling)
        project(t)
    for zo in [z] + z_others:
        for yo_ in (y, 1 - y):
            t = zo * 4 + yo_ * 2 + (1 - c)
            arrive(xbuf.at[t], x_send.at[0], x_recv.at[t])
            project(t)

    rinv = lax.rsqrt(ssq[...] * (1.0 / width) + 1e-06)
    other = yo[...] * rinv
    low = other[:, 64:128].astype(BF16)
    def column(row_ref):
        return jnp.broadcast_to(row_ref[...].astype(F32), (rows, rows)).T.astype(jnp.int32)

    adapter = column(adapter_ref)
    adapter = jnp.concatenate([adapter, adapter], axis=1)
    wide = lanes((rows, 256))
    picked = (wide // 16) == adapter
    row_of = lax.broadcasted_iota(jnp.int32, (64, 256), 0)
    col_of = lanes((64, 256)) % 16

    def spread(part, offset):
        tile = (row_of == col_of + offset).astype(F32).astype(BF16)
        return jnp.where(picked, dot(part, tile), 0.0).astype(BF16)

    queries = (yq[...] * rinv + dot(spread(low, 0), qu_ref[...].reshape(256, 256))).astype(BF16)
    odd = tp % 2
    is_key = tp < 8
    kv_low = jnp.where(is_key, spread(low, 16).astype(F32), spread(low, 32).astype(F32)).astype(BF16)
    pair_cols = pl.ds(pl.multiple_of((tp // 2) * 128, 128), 128)
    kv_update = dot(kv_low, ku_ref[:, :, pair_cols].reshape(256, 128))
    kv_base = other[:, :64]
    kv_full = (jnp.concatenate([kv_base, kv_base], axis=1) + kv_update).T
    fresh[...] = jnp.where(odd == 1, kv_full[64:], kv_full[:64]).astype(BF16)
    fold_row = lax.broadcasted_iota(jnp.int32, (256, 128), 0) % 16
    fold_col = lanes((256, 128))
    key_up = ku_ref[:, :, pl.ds(pl.multiple_of(z * 128, 128), 128)].reshape(256, 128)
    factors = jnp.zeros((rows, 128), F32)
    for h in range(2):
        full = dot_nt(queries[:, h * 128 : (h + 1) * 128], key_up)
        full = jnp.where(picked, full, 0.0).astype(BF16)
        fold = (fold_col == fold_row + 16 * h).astype(F32).astype(BF16)
        factors = factors + dot(full, fold)
    mine = 4 * grp + s
    qbuf[mine, :256, :] = queries.astype(F32).T.astype(BF16)
    qbuf[mine, 256:, :] = factors.T[:32].astype(BF16)

    far = (1 - y) * 2 + c
    direct = [(grp, far), (1 - grp, s), (1 - grp, far)]
    for n, (g, j) in enumerate(direct):
        send_q(mine, n, at(g, z * 4 + j))
    send_q(mine, 3, sibling)
    head = (tp % 8) // 2
    slot = (tp // 8) * 2 + odd
    for j in range(4):
        target = head * 4 + j

        @pl.when(target != tp)
        def _():
            send(fresh, fresh_in.at[slot], f_send.at[j], f_recv.at[slot], at(grp, target))

        @pl.when(target == tp)
        def _():
            fresh_in[slot] = fresh[...]

    send_kv(2)
    for n, (g, j) in enumerate(direct):
        index = 4 * g + j
        arrive(qbuf.at[index], x_send.at[0], q_recv.at[index])
        send_q(index, 4 + n, sibling)
    for j, waited in ((s, True), (far, True), (y * 2 + 1 - c, False), (3 - s, False)):
        for g in (grp, 1 - grp):
            index = 4 * g + j
            if not waited:
                arrive(qbuf.at[index], x_send.at[0], q_recv.at[index])
            for h in range(2):
                part = pl.ds(pl.multiple_of(h * 256 + g * 128, 128), 128)
                qcol[j, :128, part] = qbuf[index, h * 128 : (h + 1) * 128, :]
                qcol[j, 128:144, part] = qbuf[index, 256 + h * 16 : 272 + h * 16, :]
        attend(z, j, True)

    def arrived(zo):
        for n2, dst in enumerate((kbuf, vbuf, dbuf)):
            arrive(dst.at[zo], x_send.at[0], kv_recv.at[zo * 3 + n2])

    for zo in z_others[:2]:
        arrived(zo)
        augment(zo)

        def body(j, carry):
            attend(zo, j, False)
            return carry

        lax.fori_loop(0, 4, body, 0)

    arrived(z_others[2])
    augment(z_others[2])

    def last(shift, carry):
        j = (s + shift) % 4
        attend(z_others[2], j, False)
        line = lax.broadcasted_iota(jnp.int32, (16, 128), 0)
        for g in range(2):
            for h in range(2):
                part = pl.ds(h * 256 + g * 128, 128)
                psend[j, g, h * 128 : (h + 1) * 128, :] = acc[j, :128, part].astype(BF16)
                psend[j, g, 256 + h * 32 : 272 + h * 32, :] = acc[j, 128:144, part].astype(BF16)
                stats = jnp.zeros((16, 128), F32)
                pieces = split_three(acc[j, 144:145, part])[:2] + split_three(peak[j, :, part])
                for i, piece in enumerate(pieces):
                    stats = jnp.where(line == i, piece, stats)
                psend[j, g, 272 + h * 32 : 288 + h * 32, :] = stats.astype(BF16)
            here = jnp.logical_and(j == s, grp == g)

            @pl.when(jnp.logical_not(here))
            def _():
                send(psend.at[j, g], pbuf.at[mine], p_send.at[j * 2 + g], p_recv.at[mine], at(g, z * 4 + j))

            @pl.when(here)
            def _():
                pbuf[mine] = psend[j, g]

        return carry

    lax.fori_loop(1, 5, last, 0)

    for n in range(4):
        source = (n // 2) * 8 + 2 * z + n % 2

        @pl.when(source != tp)
        def _():
            arrive(fresh_in.at[n], x_send.at[0], f_recv.at[n])

    own_key = jnp.concatenate([fresh_in[0], fresh_in[1]], axis=0).astype(F32)
    own_value = jnp.concatenate([fresh_in[2], fresh_in[3]], axis=0).astype(F32)
    for n in range(1, 8):
        index = (mine + n) % 8
        arrive(pbuf.at[index], x_send.at[0], p_recv.at[index])
    half = slots_ref.shape[1]
    holder = jnp.where(doc_ref[...] == 0, slots_ref[0, 0] // half, slots_ref[1, 0] // half)
    picked = lax.broadcasted_iota(jnp.int32, (256, rows), 0) // 16 == adapter_ref[...]
    blocks = [
        jnp.where(holder == 0, pbuf[j].astype(F32), pbuf[4 + j].astype(F32)) for j in range(4)
    ]
    for h in range(2):
        query = qbuf[mine, h * 128 : (h + 1) * 128, :].astype(F32)
        own = jnp.sum(query * own_key, axis=0, keepdims=True) * scale
        base = 256 + h * 32
        peaks = [b[base + 18 : base + 19] + b[base + 19 : base + 20] + b[base + 20 : base + 21] for b in blocks]
        top = own
        for m in peaks:
            top = jnp.maximum(top, m)
        total = jnp.exp2(own - top)
        numerator = total * own_value
        factor = jnp.zeros((16, rows), F32)
        for block, m in zip(blocks, peaks):
            weight = jnp.exp2(m - top)
            numerator = numerator + block[h * 128 : (h + 1) * 128] * weight
            factor = factor + block[base : base + 16] * weight
            total = total + (block[base + 16 : base + 17] + block[base + 17 : base + 18]) * weight
        expanded = jnp.where(picked, jnp.concatenate([factor] * 16, axis=0), 0.0)
        high = expanded.astype(BF16)
        shift = dot(vup[...], high) + dot(vup[...], (expanded - high.astype(F32)).astype(BF16))
        out_ref[:, h * 128 : (h + 1) * 128] = ((numerator + shift) / total).T.astype(BF16)

    for copy in started:
        copy.wait_send()
    for j in range(4):
        target = head * 4 + j

        @pl.when(target != tp)
        def _():
            pltpu.make_async_remote_copy(
                src_ref=fresh, dst_ref=fresh_in.at[slot], send_sem=f_send.at[j],
                recv_sem=f_recv.at[slot], device_id=at(grp, target), device_id_type=MESH,
            ).wait_send()

    for j in range(4):
        for g in range(2):

            @pl.when(jnp.logical_not(jnp.logical_and(j == s, grp == g)))
            def _():
                pltpu.make_async_remote_copy(
                    src_ref=psend.at[j, g], dst_ref=pbuf.at[mine], send_sem=p_send.at[j * 2 + g],
                    recv_sem=p_recv.at[mine], device_id=at(g, z * 4 + j), device_id_type=MESH,
                ).wait_send()


def fused_device(
    residual_input, input_norm_gain, query_weight, key_value_weight, shared_down_factors,
    query_up_factors, key_value_up_factors, paged_base_keys, paged_base_values,
    paged_down_factors, adapter_of_row, document_of_row, document_page_slots,
):
    rows, chunk = residual_input.shape
    vmem = pl.BlockSpec(memory_space=pltpu.VMEM)
    hbm = pl.BlockSpec(memory_space=pltpu.HBM)
    smem = pl.BlockSpec(memory_space=pltpu.SMEM)
    dma = pltpu.SemaphoreType.DMA
    width = 16 * chunk
    return pl.pallas_call(
        fused_kernel,
        out_shape=jax.ShapeDtypeStruct((rows, 256), BF16),
        in_specs=[vmem, vmem, hbm, hbm, hbm, hbm, hbm, hbm, hbm, vmem, vmem, vmem, smem],
        out_specs=vmem,
        scratch_shapes=[
            pltpu.VMEM((16, rows, 384), BF16),
            pltpu.VMEM((width, 256), BF16),
            pltpu.VMEM((64, width), BF16),
            pltpu.VMEM((48, width), BF16),
            pltpu.VMEM((16, 16, 256), BF16),
            pltpu.VMEM((16, 16, 1024), BF16),
            pltpu.VMEM((width, 128), BF16),
            pltpu.VMEM((rows, 256), F32),
            pltpu.VMEM((rows, 128), F32),
            pltpu.VMEM((rows, 1), F32),
            pltpu.VMEM((4, 4, 128, 128), BF16),
            pltpu.VMEM((4, 4, 128, 128), BF16),
            pltpu.VMEM((4, 128, 128), BF16),
            pltpu.VMEM((8, 288, rows), BF16),
            pltpu.VMEM((4, 256, 4 * rows), BF16),
            pltpu.VMEM((4, 512, 256), BF16),
            pltpu.VMEM((4, 160, 512), BF16),
            pltpu.VMEM((128, 256), BF16),
            pltpu.VMEM((4, 160, 4 * rows), F32),
            pltpu.VMEM((4, 1, 4 * rows), F32),
            pltpu.VMEM((4, 2, 320, rows), BF16),
            pltpu.VMEM((8, 320, rows), BF16),
            pltpu.VMEM((64, rows), BF16),
            pltpu.VMEM((4, 64, rows), BF16),
            dma((7,)), dma((16,)), dma((16,)), dma((9,)), dma((12,)),
            dma((7,)), dma((8,)), dma((4,)), dma((4,)), dma((8,)), dma((8,)),
        ],
        compiler_params=pltpu.CompilerParams(
            collective_id=0, has_side_effects=True, vmem_limit_bytes=63 * 1024 * 1024
        ),
        cost_estimate=pl.CostEstimate(
            flops=5_000_000_000, bytes_accessed=8_000_000, transcendentals=4_500_000
        ),
    )(
        residual_input.T, input_norm_gain.reshape(1, width), query_weight, key_value_weight.T,
        shared_down_factors.T, query_up_factors, key_value_up_factors, paged_base_keys,
        paged_base_values, paged_down_factors.transpose(0, 2, 1), adapter_of_row.reshape(1, rows),
        document_of_row.reshape(1, rows), document_page_slots,
    )


def merge_slices(numerator, factor_sum, maxima, totals):
    peak_all = jnp.max(maxima, axis=-1)
    weight = jnp.exp(maxima - peak_all[..., None])
    numerator = jnp.sum(numerator * weight[..., None], axis=-2)
    factor_sum = jnp.sum(factor_sum * weight[..., None], axis=-2)
    totals = jnp.sum(totals * weight, axis=-1)
    return (numerator, factor_sum, peak_all, totals)


def attend_local(
    query_matrix,
    down_factors,
    paged_base_keys,
    paged_base_values,
    paged_down_factors,
    heads_kv,
    low_rank_width,
):
    item_count = query_matrix.shape[0]
    head_size = paged_base_keys.shape[-1] // heads_kv
    all_heads = query_matrix.shape[1] // head_size
    query_group_size = all_heads // heads_kv
    local_tokens = paged_base_keys.shape[0] * paged_base_keys.shape[1]
    score_scaling = head_size ** (-0.5)
    key_heads = paged_base_keys.reshape(local_tokens, heads_kv, head_size).transpose(1, 0, 2)
    value_heads = paged_base_values.reshape(local_tokens, heads_kv, head_size).transpose(1, 0, 2)
    factor_flat = paged_down_factors.reshape(local_tokens, 2 * low_rank_width)
    cached_key = factor_flat[:, :low_rank_width]
    cached_value = factor_flat[:, low_rank_width:]
    query_head_count = query_matrix.reshape(
        item_count, heads_kv, query_group_size, head_size
    ).transpose(1, 0, 2, 3)
    factor_heads = down_factors.reshape(
        item_count, heads_kv, query_group_size, low_rank_width
    ).transpose(1, 0, 2, 3)

    def one_head(bundle):
        query_one, factor_one, key_one, value_one = bundle
        scores = (
            jnp.einsum("ngd,ld->ngl", query_one, key_one, preferred_element_type=jnp.float32)
            + jnp.einsum("ngj,lj->ngl", factor_one, cached_key, preferred_element_type=jnp.float32)
        ) * score_scaling
        maxima = jnp.max(scores, -1)
        weights = jnp.exp(scores - maxima[..., None])
        totals = jnp.sum(weights, -1)
        rounded = weights.astype(jnp.bfloat16)
        numerator = jnp.einsum(
            "ngl,ld->ngd", rounded, value_one, preferred_element_type=jnp.float32
        )
        factor_sum = jnp.einsum(
            "ngl,lj->ngj", rounded, cached_value, preferred_element_type=jnp.float32
        )
        return (numerator, factor_sum, maxima, totals)

    numerator, factor_sum, maxima, totals = lax.map(
        one_head, (query_head_count, factor_heads, key_heads, value_heads)
    )
    numerator = numerator.transpose(1, 0, 2, 3).reshape(item_count, all_heads, head_size)
    factor_sum = factor_sum.transpose(1, 0, 2, 3).reshape(item_count, all_heads, low_rank_width)
    maxima = maxima.transpose(1, 0, 2).reshape(item_count, all_heads)
    totals = totals.transpose(1, 0, 2).reshape(item_count, all_heads)
    return (numerator, factor_sum, maxima, totals)


def per_device(
    residual_input,
    input_norm_gain,
    query_weight,
    key_value_weight,
    shared_down_factors,
    query_up_factors,
    key_value_up_factors,
    paged_base_keys,
    paged_base_values,
    paged_down_factors,
    adapter_of_row,
    document_of_row,
    document_page_slots,
):
    tp_count = lax.axis_size("tp")
    grp_count = lax.axis_size("grp")
    tp_index = lax.axis_index("tp")
    low_rank_width = shared_down_factors.shape[1] // 3
    key_value_width = key_value_up_factors.shape[2] // 2
    head_size = HEAD_SIZE
    heads_kv = key_value_width // head_size
    row_count = residual_input.shape[0]
    score_scaling = head_size ** (-0.5)
    gathered = lax.all_gather(residual_input, "tp", axis=1, tiled=True).astype(jnp.float32)
    normed_input = (
        gathered
        * lax.rsqrt(jnp.mean(gathered * gathered, -1, keepdims=True) + 1e-06)
        * input_norm_gain
    ).astype(jnp.bfloat16)
    low_rank_part = jnp.dot(
        normed_input, shared_down_factors, preferred_element_type=jnp.float32
    ).astype(jnp.bfloat16)
    query_low_rank = low_rank_part[:, :low_rank_width]
    key_low_rank = low_rank_part[:, low_rank_width : 2 * low_rank_width]
    value_low_rank = low_rank_part[:, 2 * low_rank_width :]
    query_update = query_up_factors[adapter_of_row]
    query_part = (
        jnp.dot(normed_input, query_weight, preferred_element_type=jnp.float32)
        + jnp.einsum("ep,epg->eg", query_low_rank, query_update, preferred_element_type=jnp.float32)
    ).astype(jnp.bfloat16)
    key_value_columns = key_value_weight.shape[1]
    key_value_start = tp_index * key_value_columns
    key_value_update = lax.dynamic_slice_in_dim(
        key_value_up_factors, key_value_start, key_value_columns, 2
    )[adapter_of_row]
    key_value_low = jnp.where(key_value_start < key_value_width, key_low_rank, value_low_rank)
    kv_part = (
        jnp.dot(normed_input, key_value_weight, preferred_element_type=jnp.float32)
        + jnp.einsum(
            "ep,epg->eg", key_value_low, key_value_update, preferred_element_type=jnp.float32
        )
    ).astype(jnp.bfloat16)
    heads_here = query_part.shape[1] // head_size
    query_group_size = heads_here * tp_count // heads_kv
    key_value_head = tp_index * heads_here // query_group_size
    key_column_count = lax.dynamic_slice_in_dim(
        key_value_up_factors, key_value_head * head_size, head_size, 2
    )[adapter_of_row]
    my_queries = query_part.reshape(row_count, heads_here, head_size)
    factor_part = jnp.einsum(
        "rhd,rjd->rhj", my_queries, key_column_count, preferred_element_type=jnp.float32
    ).astype(jnp.bfloat16)
    factor_part = factor_part.reshape(row_count, heads_here * low_rank_width)
    query_matrix, down_factors, fresh_kv = (
        lax.all_gather(query_part, "tp", axis=1, tiled=True),
        lax.all_gather(factor_part, "tp", axis=1, tiled=True),
        lax.all_gather(kv_part, "tp", axis=1, tiled=True),
    )
    doc_pages = document_page_slots.shape[1]
    owner_of_doc = document_page_slots[:, 0] // doc_pages
    doc_ids = document_of_row[:, 0]
    doc_match = (doc_ids[:, None] == jnp.arange(document_page_slots.shape[0])[None, :]).astype(
        jnp.int32
    )
    target = jnp.sum(doc_match * owner_of_doc[None, :], 1)
    target_match = (target[:, None] == jnp.arange(grp_count)[None, :]).astype(jnp.int32)
    earlier = jnp.cumsum(target_match, 0) - target_match
    capacity = 2 * row_count // grp_count
    slot_of = target * capacity + jnp.sum(earlier * target_match, 1)
    placing = (jnp.arange(grp_count * capacity)[:, None] == slot_of[None, :]).astype(jnp.bfloat16)
    send_queries = (
        jnp.dot(placing, query_matrix, preferred_element_type=jnp.float32)
        .astype(jnp.bfloat16)
        .reshape(grp_count, capacity, -1)
    )
    send_factors = (
        jnp.dot(placing, down_factors, preferred_element_type=jnp.float32)
        .astype(jnp.bfloat16)
        .reshape(grp_count, capacity, -1)
    )
    query_in = lax.all_to_all(send_queries, "grp", split_axis=0, concat_axis=0, tiled=True)
    factor_in = lax.all_to_all(send_factors, "grp", split_axis=0, concat_axis=0, tiled=True)
    per_source = query_in.shape[1]
    item_count = query_in.shape[0] * per_source
    query_flat = query_in.reshape(item_count, -1)
    factor_flat = factor_in.reshape(item_count, -1)
    numerator, factor_sum, maxima, totals = attend_local(
        query_flat,
        factor_flat,
        paged_base_keys,
        paged_base_values,
        paged_down_factors,
        heads_kv,
        low_rank_width,
    )
    all_heads = numerator.shape[1]
    returned = (
        lax.all_to_all(
            numerator.reshape(grp_count, per_source, all_heads, head_size),
            "grp",
            split_axis=0,
            concat_axis=0,
            tiled=True,
        ),
        lax.all_to_all(
            factor_sum.reshape(grp_count, per_source, all_heads, low_rank_width),
            "grp",
            split_axis=0,
            concat_axis=0,
            tiled=True,
        ),
        lax.all_to_all(
            maxima.reshape(grp_count, per_source, all_heads),
            "grp",
            split_axis=0,
            concat_axis=0,
            tiled=True,
        ),
        lax.all_to_all(
            totals.reshape(grp_count, per_source, all_heads),
            "grp",
            split_axis=0,
            concat_axis=0,
            tiled=True,
        ),
    )
    numerator, factor_sum, maxima, totals = [
        piece.reshape((grp_count * capacity,) + piece.shape[2:])[slot_of] for piece in returned
    ]
    numerator, factor_sum, maxima, totals = (
        lax.all_to_all(numerator[:, :, None, :], "tp", split_axis=1, concat_axis=2, tiled=True),
        lax.all_to_all(factor_sum[:, :, None, :], "tp", split_axis=1, concat_axis=2, tiled=True),
        lax.all_to_all(maxima[:, :, None], "tp", split_axis=1, concat_axis=2, tiled=True),
        lax.all_to_all(totals[:, :, None], "tp", split_axis=1, concat_axis=2, tiled=True),
    )
    numerator, factor_sum, maxima, totals = merge_slices(numerator, factor_sum, maxima, totals)
    own_key = lax.dynamic_slice_in_dim(fresh_kv, key_value_head * head_size, head_size, 1)
    value_own = lax.dynamic_slice_in_dim(
        fresh_kv, key_value_width + key_value_head * head_size, head_size, 1
    )
    own_token_score = (
        jnp.einsum("rhd,rd->rh", my_queries, own_key, preferred_element_type=jnp.float32)
        * score_scaling
    )
    peak_all = jnp.maximum(maxima, own_token_score)
    old_scale = jnp.exp(maxima - peak_all)
    own_weight = jnp.exp(own_token_score - peak_all)
    numerator = (
        numerator * old_scale[..., None]
        + own_weight[..., None] * value_own.astype(jnp.float32)[:, None, :]
    )
    factor_sum = factor_sum * old_scale[..., None]
    totals = totals * old_scale + own_weight
    value_column_count = lax.dynamic_slice_in_dim(
        key_value_up_factors, key_value_width + key_value_head * head_size, head_size, 2
    )[adapter_of_row]
    value_shift = jnp.einsum(
        "rhj,rjd->rhd",
        factor_sum,
        value_column_count.astype(jnp.float32),
        precision=lax.Precision.HIGHEST,
    )
    result = ((numerator + value_shift) / totals[..., None]).astype(jnp.bfloat16)
    return result.reshape(row_count, heads_here * head_size)


def solution(mesh):
    in_specs = (
        P("grp", "tp"),
        P(),
        P(None, "tp"),
        P(None, "tp"),
        P(),
        P(None, None, "tp"),
        P(),
        P(("grp", "tp"), None, None),
        P(("grp", "tp"), None, None),
        P(("grp", "tp"), None, None),
        P("grp"),
        P("grp", None),
        P(),
    )
    out_specs = P("grp", "tp")
    fits = mesh.shape["grp"] == 2 and mesh.shape["tp"] == 16
    return jax.shard_map(
        fused_device if fits else per_device, mesh=mesh, in_specs=in_specs, out_specs=out_specs, check_vma=False
    )
```
